32 devices in a mesh: samp: 4 (over z), row: 4 (over y, x), col: 2 (over core).
Axes of the slice: x: 2, y: 2, z: 4, core: 2. Of those that a mesh axis runs over, the one named last changes fastest.
Arguments:
- genotypes: int32 [2048, 2048], P('samp', 'row'), may hold values from 0 to 2, as said below
- frequencies: float32 [2048], P('row'), may hold values from 0.25 to 0.5, as said below
- trait_scores: float32 [64, 2048], P(None, 'row'), may hold values from -6 to 6
- typed_mask: int32 [2048], P('row'), may hold values 0 or 1
- panel_index: int32 [1], replicated, may hold values from 0 to 127
Outputs:
- conditioned: float32 [2048, 2048], P('row', 'col')
- whitened: float32 [64, 1024], replicated
- residual: float32 [64, 2048], P(None, 'row')
The draws below stay inside these ranges and needn't reach their ends.
Inputs may be any that keep to these rules, and one draw needn't show every extreme that they name: `genotypes`: each sample's dosage at a variant is its number of the variant's allele over two haplotypes, with the allele's chance the variant's frequency. frequencies are multiples of 1/64.
All inputs are finite; a program needn't handle non-finite values. No bound on the sum of `typed_mask` on one device may be relied on, other than what follows from the above.
Results may differ from the reference program's by a relative error of at most 0.0045.
Values may be sent and summed in bfloat16 or wider, within the bound.
No kernel may reach another device: no remote copies, remote signals or barrier semaphores. Data moves between devices by JAX's collectives and lax.ppermute only.
A program may use at most 64 MiB of HBM per device.

```python
import jax
import jax.numpy as jnp
from jax import lax

B = 1024
TRAITS = 64
V = 2048
SAMPLES = 2048
N_COL = 2


block_span = 32


def allele_levels(key):
    return jax.random.randint(jax.random.fold_in(key, 11), (V,), 16, 33)


def draw_frequencies(key, part):
    return allele_levels(key).astype(jnp.float32) / 64.0


def haplotype_alleles(key, levels, which):
    blocks = V // block_span
    shared = jax.random.randint(jax.random.fold_in(key, 20 + which), (SAMPLES, blocks), 0, 64)
    shared_full = jnp.repeat(shared, block_span, axis=1)
    own = jax.random.randint(jax.random.fold_in(key, 30 + which), (SAMPLES, V), 0, 64)
    mixing = jax.random.randint(jax.random.fold_in(key, 40 + which), (SAMPLES, V), 0, 10)
    draws = jnp.where(mixing < 9, shared_full, own)
    return (draws < levels[None, :]).astype(jnp.int32)


def draw_genotypes(key, part):
    levels = allele_levels(key)
    first = haplotype_alleles(key, levels, 0)
    second = haplotype_alleles(key, levels, 1)
    return (first + second).astype(jnp.int32)


def place_ends(entries, own_key, low, high):
    longest = entries.shape.index(max(entries.shape))
    spots = []
    for shift in (0, 1):
        where = [jax.random.randint(jax.random.fold_in(own_key, axis), (), 0, length) for axis, length in enumerate(entries.shape)]
        where[longest] = (where[longest] + shift) % entries.shape[longest]
        spots.append(tuple(where))
    return entries.at[spots[0]].set(low).at[spots[1]].set(high)


def level_of(stream_key, extent, shards, low, high):
    factor_of = 1.0
    for dim, shards_of in shards:
        steps = jax.random.uniform(jax.random.fold_in(jax.random.fold_in(stream_key, 6), dim), (shards_of,), jnp.float32, low / len(shards), high / len(shards))
        factor_of = factor_of * jnp.repeat(jnp.exp(steps), extent[dim] // shards_of).reshape((-1,) + (1,) * (len(extent) - 1 - dim))
    return factor_of


def bell_draw(rng, extent, deviation, reach, pieces=(), kind=jnp.bfloat16):
    result = deviation * jax.random.normal(rng, extent, jnp.float32)
    if pieces:
        result = result * level_of(rng, extent, pieces, -0.22, 0.18)
    return jnp.clip(result, -reach, reach).astype(kind)


def setup_inputs(seed: int = 0) -> dict:
    splits = jax.random.split(jax.random.key(seed), 6)
    genotypes = draw_genotypes(jax.random.fold_in(splits[5], 71), 0)
    frequencies = draw_frequencies(jax.random.fold_in(splits[5], 71), 0)
    trait_scores = bell_draw(splits[2], (TRAITS, V), 1.0, 6.0, ((1, 4),), jnp.float32)
    typed_mask = place_ends((jax.random.randint(splits[3], (V,), 0, 4) < 3).astype(jnp.int32), jax.random.fold_in(splits[3], 1), 0, 1)
    panel_index = jax.random.randint(splits[4], (1,), 0, 64 * N_COL).astype(jnp.int32)
    return dict(genotypes=genotypes, frequencies=frequencies, trait_scores=trait_scores, typed_mask=typed_mask, panel_index=panel_index)


ridge = 0.1

def reference(genotypes, frequencies, trait_scores, typed_mask, panel_index):
    spread = jnp.sqrt(2.0 * frequencies * (1.0 - frequencies))
    standard = ((genotypes.astype(jnp.float32) - 2.0 * frequencies) / spread).astype(jnp.bfloat16)
    values = standard.astype(jnp.float32)
    linkage = jnp.dot(values.T, values, precision=lax.Precision.HIGHEST) / SAMPLES
    linkage = linkage + ridge * jnp.eye(V, dtype=jnp.float32)
    start = (panel_index[0] % N_COL * B).astype(jnp.int32)
    panel_slab = lax.dynamic_slice_in_dim(linkage, start, B, 1)
    diag_block = lax.dynamic_slice_in_dim(panel_slab, start, B, 0)
    factor = jnp.linalg.cholesky(diag_block)
    panel_factor = lax.linalg.triangular_solve(factor, panel_slab, left_side=False, lower=True, transpose_a=True)
    conditioned = linkage - jnp.dot(panel_factor, panel_factor.T, precision=lax.Precision.HIGHEST)
    masked = trait_scores * typed_mask.astype(jnp.float32)
    masked_panel = lax.dynamic_slice_in_dim(masked, start, B, 1)
    whitened = lax.linalg.triangular_solve(factor, masked_panel, left_side=False, lower=True, transpose_a=True)
    residual = masked - jnp.dot(whitened, panel_factor.T, precision=lax.Precision.HIGHEST)
    return (conditioned, whitened, residual)
```

```python
import functools

import jax
import jax.numpy as jnp
from jax import lax
from jax.experimental import pallas as pl
from jax.experimental.pallas import tpu as pltpu
from jax.sharding import Mesh
from jax.sharding import PartitionSpec as P

ridge = 0.1
F32 = jnp.float32
BF16 = jnp.bfloat16
NN = (((1,), (0,)), ((), ()))
NT = (((1,), (1,)), ((), ()))
block = 128
sublanes = 8
vmem_bytes = 58 * 2**20


def dot1(a, b, dims):
    return lax.dot_general(a, b, dims, preferred_element_type=F32)


def split(x):
    high = x.astype(BF16)
    return high, (x - high.astype(F32)).astype(BF16)


def dot3(a, b, dims):
    return dot1(a[0], b[0], dims) + (dot1(a[0], b[1], dims) + dot1(a[1], b[0], dims))


def row_to_all(v, i):
    return jnp.broadcast_to(v[i : i + 1, :], (sublanes, block))


def lane_to_all(v, j):
    return jnp.broadcast_to(v[:, j : j + 1], (sublanes, block))


def take_away(base, coefs, rows):
    t = [c * r for c, r in zip(coefs, rows)]
    return base - (((t[0] + t[1]) + (t[2] + t[3])) + ((t[4] + t[5]) + (t[6] + t[7])))


def inverse_factor(rows):
    count = block // sublanes
    sub = lax.broadcasted_iota(jnp.int32, (sublanes, block), 0)
    lane = lax.broadcasted_iota(jnp.int32, (sublanes, block), 1)
    rows = list(rows)
    out = []
    diag = [lane_to_all(rows[0], j) for j in range(sublanes)]
    for p in range(count):
        first = sublanes * p
        inside = (lane >= first) & (lane < first + sublanes)
        work = jnp.where(inside, jnp.where(lane - first == sub, 1.0, 0.0), rows[p])
        below = {g: [lane_to_all(rows[g], first + j) for j in range(sublanes)] for g in range(p + 1, count)}
        ahead, after = [], []
        if p + 1 < count:
            nxt = first + sublanes
            ahead = [lane_to_all(rows[p], nxt + m) for m in range(sublanes)]
            after = [lane_to_all(rows[p + 1], nxt + m) for m in range(sublanes)]
        done = jnp.zeros((sublanes, block), F32)
        raw = diag[0]
        for j in range(sublanes):
            pivot = row_to_all(raw, j)
            inv = 1.0 / pivot
            ratio = diag[j] * inv
            here = sub == j
            row = row_to_all(work, j)
            done = jnp.where(here, row * lax.rsqrt(pivot), done)
            work = jnp.where(here, row * inv, work - ratio * row)
            for m in range(j + 1, sublanes):
                entry = row_to_all(diag[m], j)
                left = diag[m] - ratio * entry
                if m == j + 1:
                    raw = left
                diag[m] = jnp.where(here, entry * inv, left)
            for m in range(len(ahead)):
                entry = row_to_all(ahead[m], j)
                ahead[m] = jnp.where(here, entry * inv, ahead[m] - ratio * entry)
        out.append(jnp.where(lane <= first + sub, done, 0.0))
        work_rows = [row_to_all(work, j) for j in range(sublanes)]
        if ahead:
            diag = [
                take_away(after[m], below[p + 1], [row_to_all(ahead[m], j) for j in range(sublanes)])
                for m in range(sublanes)
            ]
        for g in below:
            rows[g] = take_away(jnp.where(inside, 0.0, rows[g]), below[g], work_rows)
    return out


def invert_in_place(a, n):
    for k in range(n // block):
        here = slice(k * block, (k + 1) * block)
        groups = [
            a[k * block + sublanes * g : k * block + sublanes * (g + 1), here] for g in range(block // sublanes)
        ]
        small = jnp.concatenate(inverse_factor(groups), axis=0)
        small_parts = split(small)
        if k > 0:
            a[here, 0 : k * block] = dot3(small_parts, split(a[here, 0 : k * block]), NN)
        a[here, here] = small
        start = (k + 1) * block
        if start == n:
            break
        a[here, start:n] = jnp.zeros((block, n - start), F32)
        rest = slice(start, n)
        column = split(dot3(split(a[rest, here]), small_parts, NT))
        change = dot3(column, split(a[here, 0:start]), NN)
        a[rest, here] = -change[:, k * block :]
        if k > 0:
            a[rest, 0 : k * block] = a[rest, 0 : k * block] - change[:, : k * block]
        for i0 in range(start, n, 2 * block):
            i1 = min(i0 + 2 * block, n)
            left = tuple(v[i0 - start : i1 - start] for v in column)
            right = tuple(v[0 : i1 - start] for v in column)
            a[i0:i1, start:i1] = a[i0:i1, start:i1] - dot3(left, right, NT)


def panel_kernel(plan, samples_all, places, *refs):
    count = len(plan)
    pieces, (inverse_ref, panel_ref, data, in_sem, out_sem) = refs[:count], refs[count:]
    width, samples = data.shape
    copies = []
    for i, (piece, slots) in enumerate(zip(pieces, plan)):
        high, depth = piece.shape[1:]
        place = pl.multiple_of(places[i], block)
        for t, slot in enumerate(slots):
            at = pl.multiple_of(places[count + slot] * depth, block)
            copies.append(
                pltpu.make_async_copy(piece.at[t], data.at[pl.ds(place, high), pl.ds(at, depth)], in_sem)
            )
    for c in copies:
        c.start()
    for c in copies:
        c.wait()
    keep = pltpu.make_async_copy(data, panel_ref, out_sem)
    keep.start()
    step = 2 * block
    for i0 in range(0, width, step):
        i1 = i0 + step
        part = dot1(data[i0:i1, :], data[0:i1, :], NT) / samples_all
        at = lax.broadcasted_iota(jnp.int32, (step, i1), 0) + i0
        across = lax.broadcasted_iota(jnp.int32, (step, i1), 1)
        inverse_ref[i0:i1, 0:i1] = part + jnp.where(at == across, ridge, 0.0)
    invert_in_place(inverse_ref, width)
    keep.wait()


def panel_step(pieces, plan, places, width, samples, samples_all):
    return pl.pallas_call(
        functools.partial(panel_kernel, plan, samples_all),
        out_shape=(
            jax.ShapeDtypeStruct((width, width), F32),
            jax.ShapeDtypeStruct((width, samples), BF16),
        ),
        in_specs=[pl.BlockSpec(memory_space=pltpu.SMEM)] + [pl.BlockSpec(memory_space=pl.ANY)] * len(pieces),
        out_specs=(pl.BlockSpec(memory_space=pltpu.VMEM), pl.BlockSpec(memory_space=pl.ANY)),
        scratch_shapes=[
            pltpu.VMEM((width, samples), BF16),
            pltpu.SemaphoreType.DMA,
            pltpu.SemaphoreType.DMA,
        ],
        compiler_params=pltpu.CompilerParams(vmem_limit_bytes=vmem_bytes),
    )(places, *pieces)


def tile_kernel(
    samples_all, n_slots, facts, panel_ref, col_ref, row_ref, inverse_ref, scores_ref, own_ref,
    cond_ref, whitened_ref, residual_ref, panel, cols, rows, high, low, change, sems,
):
    width, samples = panel.shape
    local_rows = rows.shape[0]
    depth = samples // n_slots
    row_place = pl.multiple_of(facts[2], block)
    row_place_panel = pl.multiple_of(facts[3], block)
    cols_own, rows_own = facts[0] == 1, facts[1] == 1
    load_panel = pltpu.make_async_copy(panel_ref, panel, sems.at[0])
    load_panel.start()

    def col_copies():
        return [
            pltpu.make_async_copy(
                col_ref.at[t], cols.at[:, t * depth : (t + 1) * depth], sems.at[1]
            )
            for t in range(n_slots)
        ]

    def row_copies():
        return [
            pltpu.make_async_copy(
                row_ref.at[t, pl.ds(row_place, local_rows), :],
                rows.at[:, t * depth : (t + 1) * depth],
                sems.at[2],
            )
            for t in range(n_slots)
        ]

    cols_from_panel = pltpu.make_async_copy(panel_ref, cols, sems.at[1])
    rows_from_panel = pltpu.make_async_copy(
        panel_ref.at[pl.ds(row_place_panel, local_rows), :], rows, sems.at[2]
    )

    @pl.when(rows_own)
    def _():
        rows_from_panel.start()

    @pl.when(jnp.logical_not(rows_own))
    def _():
        for c in row_copies():
            c.start()

    @pl.when(cols_own)
    def _():
        cols_from_panel.start()

    @pl.when(jnp.logical_not(cols_own))
    def _():
        for c in col_copies():
            c.start()

    high[...] = inverse_ref[...].astype(BF16)
    low[...] = (inverse_ref[...] - high[...].astype(F32)).astype(BF16)
    inverse = (high, low)
    step = 2 * block
    scores = split(scores_ref[...])
    for j0 in range(0, width, step):
        j1 = j0 + step
        whitened_ref[:, j0:j1] = dot3(
            tuple(v[:, :j1] for v in scores), tuple(v[j0:j1, :j1] for v in inverse), NT
        )
    whitened = split(whitened_ref[...])
    load_panel.wait()

    @pl.when(rows_own)
    def _():
        rows_from_panel.wait()

    @pl.when(jnp.logical_not(rows_own))
    def _():
        for c in row_copies():
            c.wait()

    for r0 in range(0, local_rows, step):
        r1 = r0 + step
        slab = dot1(rows[r0:r1, :], panel[...], NT) / samples_all
        at = lax.broadcasted_iota(jnp.int32, slab.shape, 0) + (row_place_panel + r0)
        across = lax.broadcasted_iota(jnp.int32, slab.shape, 1)
        slab = split(slab + jnp.where((at == across) & rows_own, ridge, 0.0))
        factor = jnp.concatenate(
            [
                dot3(
                    tuple(v[:, : j0 + step] for v in slab),
                    tuple(v[j0 : j0 + step, : j0 + step] for v in inverse),
                    NT,
                )
                for j0 in range(0, width, step)
            ],
            axis=1,
        )
        factor = split(factor)
        residual_ref[:, r0:r1] = own_ref[:, r0:r1] - dot3(whitened, factor, NT)
        weights = jnp.concatenate(
            [
                dot3(
                    tuple(v[:, j0:] for v in factor),
                    tuple(v[j0:, j0 : j0 + step] for v in inverse),
                    NN,
                )
                for j0 in range(0, width, step)
            ],
            axis=1,
        )
        parts = split(weights)
        explained = dot1(parts[0], panel[...], NN) + dot1(parts[1], panel[...], NN)
        change[r0:r1, :] = (rows[r0:r1, :].astype(F32) - explained).astype(BF16)
        cond_ref[r0:r1, :] = weights

    @pl.when(cols_own)
    def _():
        cols_from_panel.wait()

    @pl.when(jnp.logical_not(cols_own))
    def _():
        for c in col_copies():
            c.wait()

    row_first, col_first = facts[4], facts[5]
    for r0 in range(0, local_rows, step):
        r1 = r0 + step
        part = dot1(change[r0:r1, :], cols[...], NT) / samples_all
        at = lax.broadcasted_iota(jnp.int32, part.shape, 0) + (row_first + r0)
        across = lax.broadcasted_iota(jnp.int32, part.shape, 1) + col_first
        unit = jnp.where(at == across, 1.0, 0.0)
        cond_ref[r0:r1, :] = part + ridge * (unit - jnp.where(cols_own, cond_ref[r0:r1, :], 0.0))


def tile_step(facts, panel, col_data, row_data, inverse, scores, own, local_rows, samples_all, n_slots):
    width, samples = panel.shape
    traits = scores.shape[0]
    smem = pl.BlockSpec(memory_space=pltpu.SMEM)
    vmem = pl.BlockSpec(memory_space=pltpu.VMEM)
    anywhere = pl.BlockSpec(memory_space=pl.ANY)
    return pl.pallas_call(
        functools.partial(tile_kernel, samples_all, n_slots),
        out_shape=(
            jax.ShapeDtypeStruct((local_rows, width), F32),
            jax.ShapeDtypeStruct((traits, width), F32),
            jax.ShapeDtypeStruct((traits, local_rows), F32),
        ),
        in_specs=[smem, anywhere, anywhere, anywhere, vmem, vmem, vmem],
        out_specs=(vmem, vmem, vmem),
        scratch_shapes=[
            pltpu.VMEM((width, samples), BF16),
            pltpu.VMEM((width, samples), BF16),
            pltpu.VMEM((local_rows, samples), BF16),
            pltpu.VMEM((width, width), BF16),
            pltpu.VMEM((width, width), BF16),
            pltpu.VMEM((local_rows, samples), BF16),
            pltpu.SemaphoreType.DMA((3,)),
        ],
        compiler_params=pltpu.CompilerParams(vmem_limit_bytes=vmem_bytes),
    )(facts, panel, col_data, row_data, inverse, scores, own)


swap = [(0, 1), (1, 0)]


def on_device(genotypes, frequencies, trait_scores, typed_mask, panel_index):
    n_samp, n_pan, n_mem, n_col = (lax.axis_size(a) for a in ("samp", "pan", "mem", "col"))
    samp, pan, mem, col = (lax.axis_index(a) for a in ("samp", "pan", "mem", "col"))
    depth, local_rows = genotypes.shape
    width = local_rows * n_mem
    samples_all = depth * n_samp
    q = panel_index[0] % n_col
    spread = jnp.sqrt(2.0 * frequencies * (1.0 - frequencies))
    standard = ((genotypes.astype(F32) - 2.0 * frequencies) / spread).astype(BF16).T
    masked = trait_scores * typed_mask.astype(F32)
    own_panel = pan == q
    if n_pan == 2 and n_mem == 2 and n_col == 2 and n_samp == 4:
        quarter = local_rows // 4

        def part(i, j):
            return lax.dynamic_slice_in_dim(standard, (2 * i + j) * quarter, quarter, 0)

        mine, other = part(pan, col), lax.ppermute(part(1 - pan, col), "pan", swap)
        piece = jnp.where(own_panel, mine, other)
        rest_piece = jnp.where(own_panel, other, mine)
        along = [piece] + [
            lax.ppermute(piece, "samp", [(s, (s + d) % n_samp) for s in range(n_samp)]) for d in (1, 2, 3)
        ]
        own = jnp.stack(along)
        by_mem, by_pan = lax.ppermute(own, "mem", swap), lax.ppermute(own, "pan", swap)
        far_a = lax.ppermute(by_pan[:2], "mem", swap)
        far_b = lax.ppermute(by_mem[2:], "pan", swap)
        near = [own, by_mem, by_pan, far_a, far_b]
        twin = [lax.ppermute(v, "col", swap) for v in near]
        pieces = near + twin
        plan = [(0, 1, 2, 3)] * 3 + [(0, 1), (2, 3)]
        plan = plan + plan

        def place(m, a, c):
            return (m * 4 + a * 2 + c) * quarter

        places = [
            place(m, a, c)
            for c in (col, 1 - col)
            for m, a in ((mem, pan), (1 - mem, pan), (mem, 1 - pan), (1 - mem, 1 - pan), (1 - mem, 1 - pan))
        ] + [(samp - d) % n_samp for d in range(n_samp)]
        rest = lax.all_gather(rest_piece, ("samp", "mem", "pan", "col"))
        col_data = row_data = rest.reshape(n_samp, width, depth)
        row_place = mem * local_rows
        panel_masked = jnp.where(own_panel, masked, lax.ppermute(masked, "pan", swap))
        beside = lax.ppermute(panel_masked, "mem", swap)
        pair = [jnp.where(mem == m, panel_masked, beside) for m in range(n_mem)]
        panel_scores = jnp.concatenate(pair, axis=1)
    else:
        chosen = lax.psum(jnp.where(own_panel, standard, jnp.zeros_like(standard)), "pan")
        gathered = lax.all_gather(chosen, ("samp", "mem")).reshape(n_samp, width, depth)
        pieces, plan = [gathered], [tuple(range(n_samp))]
        places = [0, *range(n_samp)]
        cross = [(i * n_col + j, j * n_col + i) for i in range(n_pan) for j in range(n_col)]
        col_block = lax.ppermute(standard, ("pan", "col"), cross)
        col_data = lax.all_gather(col_block, ("samp", "mem")).reshape(n_samp, width, depth)
        row_data = lax.all_gather(standard, "samp")
        row_place = jnp.int32(0)
        panel_masked = lax.psum(jnp.where(own_panel, masked, jnp.zeros_like(masked)), "pan")
        panel_scores = lax.all_gather(panel_masked, "mem", axis=1, tiled=True)
    places = jnp.stack([jnp.asarray(v).astype(jnp.int32) for v in places])
    inverse, panel_data = panel_step(pieces, plan, places, width, samples_all, samples_all)
    facts = [col == q, own_panel, row_place, mem * local_rows, (pan * n_mem + mem) * local_rows, col * width]
    facts = jnp.stack([jnp.asarray(f).astype(jnp.int32) for f in facts])
    return tile_step(
        facts, panel_data, col_data, row_data, inverse, panel_scores, masked, local_rows, samples_all, n_samp
    )


def solution(mesh):
    n_samp, n_row, n_col = (mesh.shape[a] for a in ("samp", "row", "col"))
    inner = Mesh(mesh.devices.reshape(n_samp, n_col, n_row // n_col, n_col), ("samp", "pan", "mem", "col"))
    row = ("pan", "mem")
    return jax.shard_map(
        on_device,
        mesh=inner,
        in_specs=(P("samp", row), P(row), P(None, row), P(row), P()),
        out_specs=(P(row, "col"), P(), P(None, row)),
        check_vma=False,
    )
```

```python
import functools

import jax
import jax.numpy as jnp
from jax import lax
from jax.experimental import pallas as pl
from jax.experimental.pallas import tpu as pltpu
from jax.sharding import Mesh
from jax.sharding import PartitionSpec as P

ridge = 0.1
F32 = jnp.float32
BF16 = jnp.bfloat16
NN = (((1,), (0,)), ((), ()))
NT = (((1,), (1,)), ((), ()))
block = 128
sublanes = 8
vmem_bytes = 58 * 2**20


def dot1(a, b, dims):
    return lax.dot_general(a, b, dims, preferred_element_type=F32)


def split(x):
    high = x.astype(BF16)
    return high, (x - high.astype(F32)).astype(BF16)


def dot3(a, b, dims):
    (along_a,), (along_b,) = dims[0]
    left = jnp.concatenate([a[0], a[0], a[1]], axis=along_a)
    right = jnp.concatenate([b[0], b[1], b[0]], axis=along_b)
    return dot1(left, right, dims)


def row_to_all(v, i):
    return jnp.broadcast_to(v[i : i + 1, :], v.shape)


def lane_to_all(v, j):
    return jnp.take_along_axis(v, jnp.full(v.shape, j, jnp.int32), axis=1)


def take_away(base, coefs, rows):
    t = [c * r for c, r in zip(coefs, rows)]
    return base - (((t[0] + t[1]) + (t[2] + t[3])) + ((t[4] + t[5]) + (t[6] + t[7])))


def inverse_factor(rows):
    count = block // sublanes
    sub = lax.broadcasted_iota(jnp.int32, (sublanes, block), 0)
    lane = lax.broadcasted_iota(jnp.int32, (sublanes, block), 1)
    rows = list(rows)
    out = []
    diag = [lane_to_all(rows[0], j) for j in range(sublanes)]
    for p in range(count):
        first = sublanes * p
        inside = (lane >= first) & (lane < first + sublanes)
        work = jnp.where(inside, jnp.where(lane - first == sub, 1.0, 0.0), rows[p])
        near = range(p + 1, min(count, p + (4 if p % 2 == 0 else 3)))
        below = {g: [lane_to_all(rows[g], first + j) for j in range(sublanes)] for g in near}
        more = p + 1 < count
        if more:
            after = [lane_to_all(rows[p + 1], first + sublanes + m) for m in range(sublanes)]
            entry_next = list(below[p + 1])
        scaled = []
        done = jnp.zeros((sublanes, block), F32)
        raw = diag[0]
        for j in range(sublanes):
            pivot = row_to_all(raw, j)
            inv = 1.0 / pivot
            ratio = diag[j] * inv
            here = sub == j
            row = row_to_all(work, j)
            done = jnp.where(here, row * lax.rsqrt(pivot), done)
            work = jnp.where(here, row * inv, work - ratio * row)
            if more:
                scaled.append(entry_next[j] * inv)
            for m in range(j + 1, sublanes):
                entry = row_to_all(diag[m], j)
                left = diag[m] - ratio * entry
                if m == j + 1:
                    raw = left
                diag[m] = jnp.where(here, entry * inv, left)
                if more:
                    entry_next[m] = entry_next[m] - scaled[j] * entry
        out.append(jnp.where(lane <= first + sub, done, 0.0))
        if more:
            diag = [
                take_away(after[m], scaled, [row_to_all(entry_next[j], m) for j in range(sublanes)])
                for m in range(sublanes)
            ]
        work_rows = [row_to_all(work, j) for j in range(sublanes)]
        for g in near:
            rows[g] = take_away(jnp.where(inside, 0.0, rows[g]), below[g], work_rows)
        if p % 2 == 0:
            before, inside_before = work, inside
            continue
        far = range(p + 3, count)
        if not far:
            continue
        tie = [lane_to_all(before, first + m) for m in range(sublanes)]
        before = take_away(jnp.where(inside, 0.0, before), tie, work_rows)
        pair = split(jnp.concatenate([before, work], axis=0))
        top, bottom = first - sublanes, block - first - sublanes
        pair = tuple(
            jnp.concatenate(
                [jnp.zeros((h, block), BF16) if v is None else v for h, v in ((top, None), (0, w), (bottom, None)) if h or v is not None],
                axis=0,
            )
            for w in pair
        )
        change = dot3(split(jnp.concatenate([rows[g] for g in far], axis=0)), pair, NN)
        for i, g in enumerate(far):
            kept = jnp.where(inside | inside_before, 0.0, rows[g])
            rows[g] = kept - change[sublanes * i : sublanes * (i + 1)]
    return out


def invert_in_place(a, n, high, low, finish):
    def rest_of(k):
        here = slice(k * block, (k + 1) * block)
        start = (k + 1) * block
        small = (high[here, here], low[here, here])
        if k > 0:
            left = split(dot3(small, split(a[here, 0 : k * block]), NN))
            high[here, 0 : k * block], low[here, 0 : k * block] = left
        if start < n:
            for v in (high, low):
                v[here, start:n] = jnp.zeros((block, n - start), BF16)
        finish(k)
        if start == n:
            return
        rest = slice(start, n)
        column = split(dot3(split(a[rest, here]), small, NT))
        for i0 in range(start, n, 2 * block):
            i1 = min(i0 + 2 * block, n)
            left = tuple(v[i0 - start : i1 - start] for v in column)
            right = tuple(v[0 : i1 - start] for v in column)
            a[i0:i1, start:i1] = a[i0:i1, start:i1] - dot3(left, right, NT)
        a[rest, here] = -dot3(column, small, NN)
        if k > 0:
            done = (high[here, 0 : k * block], low[here, 0 : k * block])
            a[rest, 0 : k * block] = a[rest, 0 : k * block] - dot3(column, done, NN)

    def step(k, carry):
        first = pl.multiple_of(k * block, block)
        here = pl.ds(first, block)
        groups = [
            a[pl.ds(pl.multiple_of(first + sublanes * g, sublanes), sublanes), here] for g in range(block // sublanes)
        ]
        high[here, here], low[here, here] = split(jnp.concatenate(inverse_factor(groups), axis=0))
        for i in range(n // block):
            pl.when(k == i)(functools.partial(rest_of, i))
        return carry

    lax.fori_loop(0, n // block, step, 0)


def panel_kernel(plan, samples_all, places, *refs):
    count = len(plan)
    pieces, (high_ref, low_ref, panel_ref, data, a, high, low, in_sem, out_sem) = refs[:count], refs[count:]
    width, samples = data.shape
    copies = []
    for i, (piece, slots) in enumerate(zip(pieces, plan)):
        tall, depth = piece.shape[1:]
        place = pl.multiple_of(places[i], block)
        for t, slot in enumerate(slots):
            at = pl.multiple_of(places[count + slot] * depth, block)
            copies.append(
                pltpu.make_async_copy(piece.at[t], data.at[pl.ds(place, tall), pl.ds(at, depth)], in_sem)
            )
    for c in copies:
        c.start()
    for c in copies:
        c.wait()
    keep = pltpu.make_async_copy(data, panel_ref, out_sem)
    keep.start()
    step = 2 * block
    for i0 in range(0, width, step):
        i1 = i0 + step
        part = dot1(data[i0:i1, :], data[0:i1, :], NT) / samples_all
        at = lax.broadcasted_iota(jnp.int32, (step, i1), 0) + i0
        across = lax.broadcasted_iota(jnp.int32, (step, i1), 1)
        a[i0:i1, 0:i1] = part + jnp.where(at == across, ridge, 0.0)

    def out_copies(k):
        here = pl.ds(k * block, block)
        return [
            pltpu.make_async_copy(source.at[here, :], target.at[here, :], out_sem)
            for source, target in ((high, high_ref), (low, low_ref))
        ]

    def finish(k):
        for c in out_copies(k):
            c.start()

    invert_in_place(a, width, high, low, finish)
    for k in range(width // block):
        for c in out_copies(k):
            c.wait()
    keep.wait()


def panel_step(pieces, plan, places, width, samples, samples_all):
    return pl.pallas_call(
        functools.partial(panel_kernel, plan, samples_all),
        out_shape=(
            jax.ShapeDtypeStruct((width, width), BF16),
            jax.ShapeDtypeStruct((width, width), BF16),
            jax.ShapeDtypeStruct((width, samples), BF16),
        ),
        in_specs=[pl.BlockSpec(memory_space=pltpu.SMEM)] + [pl.BlockSpec(memory_space=pl.ANY)] * len(pieces),
        out_specs=(pl.BlockSpec(memory_space=pl.ANY),) * 3,
        scratch_shapes=[
            pltpu.VMEM((width, samples), BF16),
            pltpu.VMEM((width, width), F32),
            pltpu.VMEM((width, width), BF16),
            pltpu.VMEM((width, width), BF16),
            pltpu.SemaphoreType.DMA,
            pltpu.SemaphoreType.DMA,
        ],
        compiler_params=pltpu.CompilerParams(vmem_limit_bytes=vmem_bytes),
        cost_estimate=pl.CostEstimate(flops=40 * 10**9, bytes_accessed=20 * 2**20, transcendentals=0),
    )(places, *pieces)


def tile_kernel(samples_all, n_places, n_scores, col_plan, row_plan, facts, panel_ref, high_ref, low_ref, own_ref, *refs):
    score_refs, refs = refs[:n_scores], refs[n_scores:]
    pieces = refs[: len(col_plan)]
    cond_ref, whitened_ref, residual_ref, panel, cols, rows, high, low, change, sems = refs[-10:]
    extra = refs[len(col_plan) : -10]
    width, samples = panel.shape
    local_rows = rows.shape[0]
    row_place_panel = pl.multiple_of(facts[2], block)
    n_facts, slot_at = 5, 5 + n_places
    cols_own, rows_own = facts[0] == 1, facts[1] == 1
    load_panel = pltpu.make_async_copy(panel_ref, panel, sems.at[0])

    def copies(piece, target, first, plan, sem):
        tall, depth = piece.shape[1:]
        found = []
        for t, place, slot in plan:
            at = pl.multiple_of((facts[n_facts + place] if place >= 0 else 0) - first, block)
            across = pl.multiple_of(facts[slot_at + slot] * depth, block)
            found.append(
                pltpu.make_async_copy(piece.at[t], target.at[pl.ds(at, tall), pl.ds(across, depth)], sem)
            )
        return found

    def col_copies():
        return [c for p, plan in zip(pieces, col_plan) for c in copies(p, cols, 0, plan, sems.at[1])]

    def row_copies():
        if extra:
            return copies(extra[0], rows, 0, row_plan[0], sems.at[2])
        return [c for p, plan in zip(pieces, row_plan) for c in copies(p, rows, facts[2], plan, sems.at[2])]

    cols_from_panel = pltpu.make_async_copy(panel_ref, cols, sems.at[1])
    rows_from_panel = pltpu.make_async_copy(
        panel_ref.at[pl.ds(row_place_panel, local_rows), :], rows, sems.at[2]
    )

    @pl.when(rows_own)
    def _():
        rows_from_panel.start()

    @pl.when(jnp.logical_not(rows_own))
    def _():
        for c in row_copies():
            c.start()

    load_panel.start()
    loads = [
        pltpu.make_async_copy(source, target, sems.at[3]) for source, target in ((high_ref, high), (low_ref, low))
    ]
    for c in loads:
        c.start()
    @pl.when(cols_own)
    def _():
        cols_from_panel.start()

    @pl.when(jnp.logical_not(cols_own))
    def _():
        for c in col_copies():
            c.start()

    inverse = (high, low)
    step = 2 * block
    load_panel.wait()

    @pl.when(rows_own)
    def _():
        rows_from_panel.wait()

    @pl.when(jnp.logical_not(rows_own))
    def _():
        for c in row_copies():
            c.wait()

    slabs = []
    for r0 in range(0, local_rows, step):
        slab = dot1(rows[r0 : r0 + step, :], panel[...], NT) / samples_all
        at = lax.broadcasted_iota(jnp.int32, slab.shape, 0) + (row_place_panel + r0)
        across = lax.broadcasted_iota(jnp.int32, slab.shape, 1)
        slabs.append(split(slab + jnp.where((at == across) & rows_own, ridge, 0.0)))
    for c in loads:
        c.wait()
    scores = score_refs[0][...]
    if n_scores == 2:
        beside = score_refs[1][...]
        first = row_place_panel == 0
        scores = jnp.concatenate([jnp.where(first, scores, beside), jnp.where(first, beside, scores)], axis=1)
    scores = split(scores)
    for j0 in range(0, width, step):
        j1 = j0 + step
        whitened_ref[:, j0:j1] = dot3(
            tuple(v[:, :j1] for v in scores), tuple(v[j0:j1, :j1] for v in inverse), NT
        )
    whitened = split(whitened_ref[...])
    for slab, r0 in zip(slabs, range(0, local_rows, step)):
        r1 = r0 + step
        factor = jnp.concatenate(
            [
                dot3(
                    tuple(v[:, : j0 + step] for v in slab),
                    tuple(v[j0 : j0 + step, : j0 + step] for v in inverse),
                    NT,
                )
                for j0 in range(0, width, step)
            ],
            axis=1,
        )
        factor = split(factor)
        residual_ref[:, r0:r1] = own_ref[:, r0:r1] - dot3(whitened, factor, NT)
        weights = jnp.concatenate(
            [
                dot3(
                    tuple(v[:, j0:] for v in factor),
                    tuple(v[j0:, j0 : j0 + step] for v in inverse),
                    NN,
                )
                for j0 in range(0, width, step)
            ],
            axis=1,
        )
        parts = split(weights)
        both = jnp.concatenate([panel[...], panel[...]], axis=0)
        explained = dot1(jnp.concatenate(parts, axis=1), both, NN)
        change[r0:r1, :] = (rows[r0:r1, :].astype(F32) - explained).astype(BF16)
        cond_ref[r0:r1, :] = weights

    @pl.when(cols_own)
    def _():
        cols_from_panel.wait()

    @pl.when(jnp.logical_not(cols_own))
    def _():
        for c in col_copies():
            c.wait()

    row_first, col_first = facts[3], facts[4]
    for r0 in range(0, local_rows, step):
        r1 = r0 + step
        part = dot1(change[r0:r1, :], cols[...], NT) / samples_all
        at = lax.broadcasted_iota(jnp.int32, part.shape, 0) + (row_first + r0)
        across = lax.broadcasted_iota(jnp.int32, part.shape, 1) + col_first
        unit = jnp.where(at == across, 1.0, 0.0)
        cond_ref[r0:r1, :] = part + ridge * (unit - jnp.where(cols_own, cond_ref[r0:r1, :], 0.0))


def tile_step(facts, panel, high, low, scores, own, pieces, n_places, col_plan, row_plan, extra, samples_all):
    width, samples = panel.shape
    traits, local_rows = own.shape
    smem = pl.BlockSpec(memory_space=pltpu.SMEM)
    vmem = pl.BlockSpec(memory_space=pltpu.VMEM)
    anywhere = pl.BlockSpec(memory_space=pl.ANY)
    return pl.pallas_call(
        functools.partial(tile_kernel, samples_all, n_places, len(scores), col_plan, row_plan),
        out_shape=(
            jax.ShapeDtypeStruct((local_rows, width), F32),
            jax.ShapeDtypeStruct((traits, width), F32),
            jax.ShapeDtypeStruct((traits, local_rows), F32),
        ),
        in_specs=[smem] + [anywhere] * 3 + [vmem] * (1 + len(scores)) + [anywhere] * (len(pieces) + len(extra)),
        out_specs=(vmem, vmem, vmem),
        scratch_shapes=[
            pltpu.VMEM((width, samples), BF16),
            pltpu.VMEM((width, samples), BF16),
            pltpu.VMEM((local_rows, samples), BF16),
            pltpu.VMEM((width, width), BF16),
            pltpu.VMEM((width, width), BF16),
            pltpu.VMEM((local_rows, samples), BF16),
            pltpu.SemaphoreType.DMA((4,)),
        ],
        compiler_params=pltpu.CompilerParams(vmem_limit_bytes=vmem_bytes),
        cost_estimate=pl.CostEstimate(flops=20 * 10**9, bytes_accessed=20 * 2**20, transcendentals=0),
    )(facts, panel, high, low, own, *scores, *pieces, *extra)


swap = [(0, 1), (1, 0)]


def on_device(genotypes, frequencies, trait_scores, typed_mask, panel_index):
    n_samp, n_pan, n_mem, n_col = (lax.axis_size(a) for a in ("samp", "pan", "mem", "col"))
    samp, pan, mem, col = (lax.axis_index(a) for a in ("samp", "pan", "mem", "col"))
    depth, local_rows = genotypes.shape
    width = local_rows * n_mem
    samples_all = depth * n_samp
    q = panel_index[0] % n_col
    spread = jnp.sqrt(2.0 * frequencies * (1.0 - frequencies))
    standard = ((genotypes.astype(F32) - 2.0 * frequencies) / spread).astype(BF16).T
    masked = trait_scores * typed_mask.astype(F32)
    own_panel = pan == q
    rest = []
    if n_pan == 2 and n_mem == 2 and n_col == 2 and n_samp == 4:
        quarter = local_rows // 4

        def part(i, j):
            return lax.dynamic_slice_in_dim(standard, (2 * i + j) * quarter, quarter, 0)

        mine, other = part(pan, col), lax.ppermute(part(1 - pan, col), "pan", swap)
        piece = jnp.where(own_panel, mine, other)
        rest_piece = jnp.where(own_panel, other, mine)

        def along_samp(v):
            steps = [[(s, (s + d) % n_samp) for s in range(n_samp)] for d in (1, 2, 3)]
            return [lax.ppermute(v, "samp", pairs) for pairs in steps]

        own = jnp.stack([piece] + along_samp(piece))
        panel_masked = jnp.where(own_panel, masked, lax.ppermute(masked, "pan", swap))
        own, panel_masked = lax.optimization_barrier((own, panel_masked))
        beside = lax.ppermute(panel_masked, "mem", swap)
        by_mem, by_pan = lax.ppermute(own, "mem", swap), lax.ppermute(own, "pan", swap)
        far_a = lax.ppermute(by_pan[:2], "mem", swap)
        far_b = lax.ppermute(by_mem[2:], "pan", swap)
        near = [own, by_mem, by_pan, far_a, far_b]
        twin = [lax.ppermute(v, "col", swap) for v in near]
        pieces = near + twin
        plan = [(0, 1, 2, 3)] * 3 + [(0, 1), (2, 3)]
        plan = plan + plan

        def place(m, a, c):
            return (m * 4 + a * 2 + c) * quarter

        slots = [(samp - d) % n_samp for d in range(n_samp)]
        corners = ((mem, pan), (1 - mem, pan), (mem, 1 - pan), (1 - mem, 1 - pan))
        places = [place(m, a, c) for c in (col, 1 - col) for m, a in corners + corners[3:]] + slots
        rest_piece, _ = lax.optimization_barrier((rest_piece, own))
        rest_own = jnp.stack([rest_piece] + along_samp(rest_piece))
        rest_own, _, _, beside = lax.optimization_barrier((rest_own, by_mem, by_pan, beside))
        cross = [(2 * i + j, 2 * (1 - i) + 1 - j) for i in range(2) for j in range(2)]
        rest = [
            rest_own,
            lax.ppermute(rest_own, "mem", swap),
            lax.ppermute(rest_own, "pan", swap),
            lax.ppermute(rest_own, ("pan", "mem"), cross),
        ]
        rest_twin = lax.ppermute(rest_own, "col", swap)
        col_plan = [[(d, t + 4 * c, d) for d in range(4)] for c in range(2) for t in range(4)]
        row_plan = [plan if i % 2 == 0 else [] for i, plan in enumerate(col_plan)]
        extra, n_places = [], 8
        col_places = [place(m, a, c) for c in (col, 1 - col) for m, a in corners] + slots
        panel_scores = [panel_masked, beside]
    else:
        chosen = lax.psum(jnp.where(own_panel, standard, jnp.zeros_like(standard)), "pan")
        gathered = lax.all_gather(chosen, ("samp", "mem")).reshape(n_samp, width, depth)
        pieces, plan = [gathered], [tuple(range(n_samp))]
        places = [0, *range(n_samp)]
        cross = [(i * n_col + j, j * n_col + i) for i in range(n_pan) for j in range(n_col)]
        col_block = lax.ppermute(standard, ("pan", "col"), cross)
        col_pieces = [lax.all_gather(col_block, ("samp", "mem")).reshape(n_samp, width, depth)]
        extra, n_places = [lax.all_gather(standard, "samp")], 1
        col_plan = [[(s, 0, s) for s in range(n_samp)]]
        row_plan = [[(s, -1, s) for s in range(n_samp)]]
        col_places = places
        panel_masked = lax.psum(jnp.where(own_panel, masked, jnp.zeros_like(masked)), "pan")
        panel_scores = [lax.all_gather(panel_masked, "mem", axis=1, tiled=True)]
    places = jnp.stack([jnp.asarray(v).astype(jnp.int32) for v in places])
    facts = [col == q, own_panel, mem * local_rows, (pan * n_mem + mem) * local_rows, col * width, *col_places]
    facts = jnp.stack([jnp.asarray(f).astype(jnp.int32) for f in facts])
    facts, places = lax.optimization_barrier((facts, places))
    high, low, panel_data = panel_step(pieces, plan, places, width, samples_all, samples_all)
    if rest:
        held = lax.optimization_barrier((high, *rest[1:]))
        high = held[0]
        rest = [rest[0], *held[1:]]
        col_pieces = rest + [rest_twin] + [lax.ppermute(v, "col", swap) for v in rest[1:]]
    return tile_step(
        facts, panel_data, high, low, panel_scores, masked, col_pieces, n_places, col_plan, row_plan, extra, samples_all
    )


def solution(mesh):
    n_samp, n_row, n_col = (mesh.shape[a] for a in ("samp", "row", "col"))
    inner = Mesh(mesh.devices.reshape(n_samp, n_col, n_row // n_col, n_col), ("samp", "pan", "mem", "col"))
    row = ("pan", "mem")
    return jax.shard_map(
        on_device,
        mesh=inner,
        in_specs=(P("samp", row), P(row), P(None, row), P(row), P()),
        out_specs=(P(row, "col"), P(), P(None, row)),
        check_vma=False,
    )
```

```python
import functools

import jax
import jax.numpy as jnp
from jax import lax
from jax.experimental import pallas as pl
from jax.experimental.pallas import tpu as pltpu
from jax.sharding import Mesh
from jax.sharding import PartitionSpec as P

ridge = 0.1
F32 = jnp.float32
BF16 = jnp.bfloat16
NN = (((1,), (0,)), ((), ()))
NT = (((1,), (1,)), ((), ()))
block = 128
sublanes = 8
vmem_bytes = 58 * 2**20


def dot1(a, b, dims):
    return lax.dot_general(a, b, dims, preferred_element_type=F32)


def split(x):
    high = x.astype(BF16)
    return high, (x - high.astype(F32)).astype(BF16)


def dot3(a, b, dims):
    (along_a,), (along_b,) = dims[0]
    left = jnp.concatenate([a[0], a[0], a[1]], axis=along_a)
    right = jnp.concatenate([b[0], b[1], b[0]], axis=along_b)
    return dot1(left, right, dims)


def row_to_all(v, i):
    return jnp.broadcast_to(v[i : i + 1, :], v.shape)


def lane_to_all(v, j):
    return jnp.take_along_axis(v, jnp.full(v.shape, j, jnp.int32), axis=1)


def take_away(base, coefs, rows):
    t = [c * r for c, r in zip(coefs, rows)]
    return base - (((t[0] + t[1]) + (t[2] + t[3])) + ((t[4] + t[5]) + (t[6] + t[7])))


def inverse_factor(rows, beside=None):
    count = block // sublanes
    sub = lax.broadcasted_iota(jnp.int32, (sublanes, block), 0)
    lane = lax.broadcasted_iota(jnp.int32, (sublanes, block), 1)
    rows = list(rows)
    out = []
    diag = [lane_to_all(rows[0], j) for j in range(sublanes)]
    for p in range(count):
        first = sublanes * p
        inside = (lane >= first) & (lane < first + sublanes)
        work = jnp.where(inside, jnp.where(lane - first == sub, 1.0, 0.0), rows[p])
        near = range(p + 1, min(count, p + (4 if p % 2 == 0 else 3)))
        below = {g: [lane_to_all(rows[g], first + j) for j in range(sublanes)] for g in near}
        more = p + 1 < count
        if more:
            after = [lane_to_all(rows[p + 1], first + sublanes + m) for m in range(sublanes)]
            entry_next = list(below[p + 1])
        scaled = []
        done = jnp.zeros((sublanes, block), F32)
        raw = diag[0]
        for j in range(sublanes):
            pivot = row_to_all(raw, j)
            inv = 1.0 / pivot
            ratio = diag[j] * inv
            here = sub == j
            row = row_to_all(work, j)
            done = jnp.where(here, row * lax.rsqrt(pivot), done)
            work = jnp.where(here, row * inv, work - ratio * row)
            if more:
                scaled.append(entry_next[j] * inv)
            for m in range(j + 1, sublanes):
                entry = row_to_all(diag[m], j)
                left = diag[m] - ratio * entry
                if m == j + 1:
                    raw = left
                diag[m] = jnp.where(here, entry * inv, left)
                if more:
                    entry_next[m] = entry_next[m] - scaled[j] * entry
        out.append(jnp.where(lane <= first + sub, done, 0.0))
        if beside is not None:
            beside(p)
        if more:
            diag = [
                take_away(after[m], scaled, [row_to_all(entry_next[j], m) for j in range(sublanes)])
                for m in range(sublanes)
            ]
        work_rows = [row_to_all(work, j) for j in range(sublanes)]
        for g in near:
            rows[g] = take_away(jnp.where(inside, 0.0, rows[g]), below[g], work_rows)
        if p % 2 == 0:
            before, inside_before = work, inside
            continue
        far = range(p + 3, count)
        if not far:
            continue
        tie = [lane_to_all(before, first + m) for m in range(sublanes)]
        before = take_away(jnp.where(inside, 0.0, before), tie, work_rows)
        pair = split(jnp.concatenate([before, work], axis=0))
        top, bottom = first - sublanes, block - first - sublanes
        pair = tuple(
            jnp.concatenate(
                [jnp.zeros((h, block), BF16) if v is None else v for h, v in ((top, None), (0, w), (bottom, None)) if h or v is not None],
                axis=0,
            )
            for w in pair
        )
        change = dot3(split(jnp.concatenate([rows[g] for g in far], axis=0)), pair, NN)
        for i, g in enumerate(far):
            kept = jnp.where(inside | inside_before, 0.0, rows[g])
            rows[g] = kept - change[sublanes * i : sublanes * (i + 1)]
    return out


def invert_in_place(a, n, corner, fill, high, low, columns, line, finish):
    def factor_of(value, beside=None):
        return split(
            jnp.concatenate(
                inverse_factor([value[sublanes * g : sublanes * (g + 1)] for g in range(block // sublanes)], beside), axis=0
            )
        )

    def make_line(k):
        first = pl.multiple_of(k * block, block)
        here = pl.ds(first, block)
        small = (high[here, here], low[here, here])
        at = lax.broadcasted_iota(jnp.int32, (block, n), 0)
        across = lax.broadcasted_iota(jnp.int32, (block, n), 1) - first
        inside = (across >= 0) & (across < block)
        given = jnp.where(inside, jnp.where(at == across, 1.0, 0.0), a[here, :])
        found = dot3(small, split(given), NN)
        high[here, :], low[here, :] = split(jnp.where(across < block, found, 0.0))
        finish(k)
        return found

    def step(k, carry):
        first = pl.multiple_of(k * block, block)
        after = pl.ds(pl.multiple_of(first + block, block), block)
        here = pl.ds(first, block)
        small = (high[here, here], low[here, here])
        left = split(dot3(split(a[after, here]), small, NT))
        corner = a[after, after] - dot3(left, left, NT)
        across = lax.broadcasted_iota(jnp.int32, (128, n), 1) - first
        inside = (across >= 0) & (across < block)
        turns = [2 * i for i in range(1, n // block)] + [n // block * 2 - 1]

        def beside(p):
            if p == 0:
                line[0], line[1] = split(make_line(k))
            if p == 1:
                columns[0], columns[1] = split(dot3(split(a[:, here]), small, NT))
            if p in turns:
                i0 = turns.index(p) * 128
                i1 = i0 + 128
                change = dot3((columns[0, i0:i1, :], columns[1, i0:i1, :]), (line[0], line[1]), NN)
                a[i0:i1, :] = jnp.where(inside, 0.0, a[i0:i1, :]) - change

        high[after, after], low[after, after] = factor_of(corner, beside)
        return carry

    high[0:block, 0:block], low[0:block, 0:block] = factor_of(corner, fill)
    lax.fori_loop(0, n // block - 1, step, 0)
    make_line(n // block - 1)


def panel_kernel(plan, samples_all, places, *refs):
    count = len(plan)
    pieces, (high_ref, low_ref, panel_ref, data, a, high, low, columns, line, in_sem, out_sem) = refs[:count], refs[count:]
    width, samples = data.shape
    copies = []
    for i, (piece, slots) in enumerate(zip(pieces, plan)):
        tall, depth = piece.shape[1:]
        place = pl.multiple_of(places[i], block)
        for t, slot in enumerate(slots):
            at = pl.multiple_of(places[count + slot] * depth, block)
            copies.append(
                pltpu.make_async_copy(piece.at[t], data.at[pl.ds(place, tall), pl.ds(at, depth)], in_sem)
            )
    for c in copies:
        c.start()
    for c in copies:
        c.wait()
    keep = pltpu.make_async_copy(data, panel_ref, out_sem)
    keep.start()
    step = 2 * block

    def linkage_rows(i0, tall, wide):
        part = dot1(data[i0 : i0 + tall, :], data[0:wide, :], NT) / samples_all
        at = lax.broadcasted_iota(jnp.int32, part.shape, 0) + i0
        across = lax.broadcasted_iota(jnp.int32, part.shape, 1)
        return part + jnp.where(at == across, ridge, 0.0)

    def fill(p):
        turns = block // sublanes * step // width
        if p % turns == 0:
            i0 = p // turns * step
            a[i0 : i0 + step, :] = linkage_rows(i0, step, width)

    def out_copies(k):
        here = pl.ds(pl.multiple_of(k * block, block), block)
        return [
            pltpu.make_async_copy(source.at[here, :], target.at[here, :], out_sem)
            for source, target in ((high, high_ref), (low, low_ref))
        ]

    def finish(k):
        for c in out_copies(k):
            c.start()

    invert_in_place(a, width, linkage_rows(0, block, block), fill, high, low, columns, line, finish)
    for k in range(width // block):
        for c in out_copies(k):
            c.wait()
    keep.wait()


def panel_step(pieces, plan, places, width, samples, samples_all):
    return pl.pallas_call(
        functools.partial(panel_kernel, plan, samples_all),
        out_shape=(
            jax.ShapeDtypeStruct((width, width), BF16),
            jax.ShapeDtypeStruct((width, width), BF16),
            jax.ShapeDtypeStruct((width, samples), BF16),
        ),
        in_specs=[pl.BlockSpec(memory_space=pltpu.SMEM)] + [pl.BlockSpec(memory_space=pl.ANY)] * len(pieces),
        out_specs=(pl.BlockSpec(memory_space=pl.ANY),) * 3,
        scratch_shapes=[
            pltpu.VMEM((width, samples), BF16),
            pltpu.VMEM((width, width), F32),
            pltpu.VMEM((width, width), BF16),
            pltpu.VMEM((width, width), BF16),
            pltpu.VMEM((2, width, block), BF16),
            pltpu.VMEM((2, block, width), BF16),
            pltpu.SemaphoreType.DMA,
            pltpu.SemaphoreType.DMA,
        ],
        compiler_params=pltpu.CompilerParams(vmem_limit_bytes=vmem_bytes),
        cost_estimate=pl.CostEstimate(flops=40 * 10**9, bytes_accessed=20 * 2**20, transcendentals=0),
    )(places, *pieces)


def tile_kernel(samples_all, n_places, n_scores, col_plan, row_plan, facts, panel_ref, high_ref, low_ref, own_ref, *refs):
    score_refs, refs = refs[:n_scores], refs[n_scores:]
    pieces = refs[: len(col_plan)]
    cond_ref, whitened_ref, residual_ref, panel, cols, rows, high, low, change, sems = refs[-10:]
    extra = refs[len(col_plan) : -10]
    width, samples = panel.shape
    local_rows = rows.shape[0]
    row_place_panel = pl.multiple_of(facts[2], block)
    n_facts, slot_at = 5, 5 + n_places
    cols_own, rows_own = facts[0] == 1, facts[1] == 1
    load_panel = pltpu.make_async_copy(panel_ref, panel, sems.at[0])

    def copies(piece, target, first, plan, sem):
        tall, depth = piece.shape[1:]
        found = []
        for t, place, slot in plan:
            at = pl.multiple_of((facts[n_facts + place] if place >= 0 else 0) - first, block)
            across = pl.multiple_of(facts[slot_at + slot] * depth, block)
            found.append(
                pltpu.make_async_copy(piece.at[t], target.at[pl.ds(at, tall), pl.ds(across, depth)], sem)
            )
        return found

    def col_copies():
        return [c for p, plan in zip(pieces, col_plan) for c in copies(p, cols, 0, plan, sems.at[1])]

    def row_copies():
        if extra:
            return copies(extra[0], rows, 0, row_plan[0], sems.at[2])
        return [c for p, plan in zip(pieces, row_plan) for c in copies(p, rows, facts[2], plan, sems.at[2])]

    cols_from_panel = pltpu.make_async_copy(panel_ref, cols, sems.at[1])
    rows_from_panel = pltpu.make_async_copy(
        panel_ref.at[pl.ds(row_place_panel, local_rows), :], rows, sems.at[2]
    )

    @pl.when(rows_own)
    def _():
        rows_from_panel.start()

    @pl.when(jnp.logical_not(rows_own))
    def _():
        for c in row_copies():
            c.start()

    load_panel.start()
    loads = [
        pltpu.make_async_copy(source, target, sems.at[3]) for source, target in ((high_ref, high), (low_ref, low))
    ]
    for c in loads:
        c.start()
    @pl.when(cols_own)
    def _():
        cols_from_panel.start()

    @pl.when(jnp.logical_not(cols_own))
    def _():
        for c in col_copies():
            c.start()

    inverse = (high, low)
    step = 2 * block
    load_panel.wait()

    @pl.when(rows_own)
    def _():
        rows_from_panel.wait()

    @pl.when(jnp.logical_not(rows_own))
    def _():
        for c in row_copies():
            c.wait()

    tall = min(256, local_rows)
    chunks = [(r0, r0 + tall) for r0 in range(0, local_rows, tall)]
    tiles = [(j0, j0 + step) for j0 in range(0, width, step)]
    slabs = []
    for r0, r1 in chunks:
        slab = dot1(rows[r0:r1, :], panel[...], NT) / samples_all
        at = lax.broadcasted_iota(jnp.int32, slab.shape, 0) + (row_place_panel + r0)
        across = lax.broadcasted_iota(jnp.int32, slab.shape, 1)
        slabs.append(split(slab + jnp.where((at == across) & rows_own, ridge, 0.0)))
    for c in loads:
        c.wait()
    factors = []
    for slab in slabs:
        parts = [
            dot3(tuple(v[:, :j1] for v in slab), tuple(v[j0:j1, :j1] for v in inverse), NT) for j0, j1 in tiles
        ]
        factors.append(split(jnp.concatenate(parts, axis=1)))
    weights = []
    for (r0, r1), factor in zip(chunks, factors):
        parts = [
            dot3(tuple(v[:, j0:] for v in factor), tuple(v[j0:, j0:j1] for v in inverse), NN) for j0, j1 in tiles
        ]
        value = jnp.concatenate(parts, axis=1)
        cond_ref[r0:r1, :] = value
        weights.append(split(value))
    scores = score_refs[0][...]
    if n_scores == 2:
        beside = score_refs[1][...]
        first = row_place_panel == 0
        scores = jnp.concatenate([jnp.where(first, scores, beside), jnp.where(first, beside, scores)], axis=1)
    scores = split(scores)
    for j0, j1 in tiles:
        whitened_ref[:, j0:j1] = dot3(
            tuple(v[:, :j1] for v in scores), tuple(v[j0:j1, :j1] for v in inverse), NT
        )
    for (r0, r1), parts in zip(chunks, weights):
        both = jnp.concatenate([panel[...], panel[...]], axis=0)
        explained = dot1(jnp.concatenate(parts, axis=1), both, NN)
        change[r0:r1, :] = (rows[r0:r1, :].astype(F32) - explained).astype(BF16)
    whitened = split(whitened_ref[...])
    for (r0, r1), factor in zip(chunks, factors):
        residual_ref[:, r0:r1] = own_ref[:, r0:r1] - dot3(whitened, factor, NT)

    @pl.when(cols_own)
    def _():
        cols_from_panel.wait()

    @pl.when(jnp.logical_not(cols_own))
    def _():
        for c in col_copies():
            c.wait()

    row_first, col_first = facts[3], facts[4]
    for r0, r1 in chunks:
        part = dot1(change[r0:r1, :], cols[...], NT) / samples_all
        at = lax.broadcasted_iota(jnp.int32, part.shape, 0) + (row_first + r0)
        across = lax.broadcasted_iota(jnp.int32, part.shape, 1) + col_first
        unit = jnp.where(at == across, 1.0, 0.0)
        cond_ref[r0:r1, :] = part + ridge * (unit - jnp.where(cols_own, cond_ref[r0:r1, :], 0.0))


def tile_step(facts, panel, high, low, scores, own, pieces, n_places, col_plan, row_plan, extra, samples_all):
    width, samples = panel.shape
    traits, local_rows = own.shape
    smem = pl.BlockSpec(memory_space=pltpu.SMEM)
    vmem = pl.BlockSpec(memory_space=pltpu.VMEM)
    anywhere = pl.BlockSpec(memory_space=pl.ANY)
    return pl.pallas_call(
        functools.partial(tile_kernel, samples_all, n_places, len(scores), col_plan, row_plan),
        out_shape=(
            jax.ShapeDtypeStruct((local_rows, width), F32),
            jax.ShapeDtypeStruct((traits, width), F32),
            jax.ShapeDtypeStruct((traits, local_rows), F32),
        ),
        in_specs=[smem] + [anywhere] * 3 + [vmem] * (1 + len(scores)) + [anywhere] * (len(pieces) + len(extra)),
        out_specs=(vmem, vmem, vmem),
        scratch_shapes=[
            pltpu.VMEM((width, samples), BF16),
            pltpu.VMEM((width, samples), BF16),
            pltpu.VMEM((local_rows, samples), BF16),
            pltpu.VMEM((width, width), BF16),
            pltpu.VMEM((width, width), BF16),
            pltpu.VMEM((local_rows, samples), BF16),
            pltpu.SemaphoreType.DMA((4,)),
        ],
        compiler_params=pltpu.CompilerParams(vmem_limit_bytes=vmem_bytes),
        cost_estimate=pl.CostEstimate(flops=20 * 10**9, bytes_accessed=20 * 2**20, transcendentals=0),
    )(facts, panel, high, low, own, *scores, *pieces, *extra)


swap = [(0, 1), (1, 0)]


def on_device(genotypes, frequencies, trait_scores, typed_mask, panel_index):
    n_samp, n_pan, n_mem, n_col = (lax.axis_size(a) for a in ("samp", "pan", "mem", "col"))
    samp, pan, mem, col = (lax.axis_index(a) for a in ("samp", "pan", "mem", "col"))
    depth, local_rows = genotypes.shape
    width = local_rows * n_mem
    samples_all = depth * n_samp
    q = panel_index[0] % n_col
    spread = jnp.sqrt(2.0 * frequencies * (1.0 - frequencies))
    standard = ((genotypes.astype(F32) - 2.0 * frequencies) / spread).astype(BF16).T
    masked = trait_scores * typed_mask.astype(F32)
    own_panel = pan == q
    rest = []
    if n_pan == 2 and n_mem == 2 and n_col == 2 and n_samp == 4:
        quarter = local_rows // 4

        def part(i, j):
            return lax.dynamic_slice_in_dim(standard, (2 * i + j) * quarter, quarter, 0)

        mine, other = part(pan, col), lax.ppermute(part(1 - pan, col), "pan", swap)
        piece = jnp.where(own_panel, mine, other)
        rest_piece = jnp.where(own_panel, other, mine)

        def along_samp(v):
            steps = [[(s, (s + d) % n_samp) for s in range(n_samp)] for d in (1, 2, 3)]
            return [lax.ppermute(v, "samp", pairs) for pairs in steps]

        own = jnp.stack([piece] + along_samp(piece))
        panel_masked = jnp.where(own_panel, masked, lax.ppermute(masked, "pan", swap))
        own, panel_masked = lax.optimization_barrier((own, panel_masked))
        beside = lax.ppermute(panel_masked, "mem", swap)
        by_mem, by_pan = lax.ppermute(own, "mem", swap), lax.ppermute(own, "pan", swap)
        far_a = lax.ppermute(by_pan[:2], "mem", swap)
        far_b = lax.ppermute(by_mem[2:], "pan", swap)
        near = [own, by_mem, by_pan, far_a, far_b]
        twin = [lax.ppermute(v, "col", swap) for v in near]
        pieces = near + twin
        plan = [(0, 1, 2, 3)] * 3 + [(0, 1), (2, 3)]
        plan = plan + plan

        def place(m, a, c):
            return (m * 4 + a * 2 + c) * quarter

        slots = [(samp - d) % n_samp for d in range(n_samp)]
        corners = ((mem, pan), (1 - mem, pan), (mem, 1 - pan), (1 - mem, 1 - pan))
        places = [place(m, a, c) for c in (col, 1 - col) for m, a in corners + corners[3:]] + slots
        rest_piece, _ = lax.optimization_barrier((rest_piece, own))
        rest_own = jnp.stack([rest_piece] + along_samp(rest_piece))
        rest_own, _, _, beside = lax.optimization_barrier((rest_own, by_mem, by_pan, beside))
        cross = [(2 * i + j, 2 * (1 - i) + 1 - j) for i in range(2) for j in range(2)]
        rest = [
            rest_own,
            lax.ppermute(rest_own, "mem", swap),
            lax.ppermute(rest_own, "pan", swap),
            lax.ppermute(rest_own, ("pan", "mem"), cross),
        ]
        rest_twin = lax.ppermute(rest_own, "col", swap)
        col_plan = [[(d, t + 4 * c, d) for d in range(4)] for c in range(2) for t in range(4)]
        row_plan = [plan if i % 2 == 0 else [] for i, plan in enumerate(col_plan)]
        extra, n_places = [], 8
        col_places = [place(m, a, c) for c in (col, 1 - col) for m, a in corners] + slots
        panel_scores = [panel_masked, beside]
    else:
        chosen = lax.psum(jnp.where(own_panel, standard, jnp.zeros_like(standard)), "pan")
        gathered = lax.all_gather(chosen, ("samp", "mem")).reshape(n_samp, width, depth)
        pieces, plan = [gathered], [tuple(range(n_samp))]
        places = [0, *range(n_samp)]
        cross = [(i * n_col + j, j * n_col + i) for i in range(n_pan) for j in range(n_col)]
        col_block = lax.ppermute(standard, ("pan", "col"), cross)
        col_pieces = [lax.all_gather(col_block, ("samp", "mem")).reshape(n_samp, width, depth)]
        extra, n_places = [lax.all_gather(standard, "samp")], 1
        col_plan = [[(s, 0, s) for s in range(n_samp)]]
        row_plan = [[(s, -1, s) for s in range(n_samp)]]
        col_places = places
        panel_masked = lax.psum(jnp.where(own_panel, masked, jnp.zeros_like(masked)), "pan")
        panel_scores = [lax.all_gather(panel_masked, "mem", axis=1, tiled=True)]
    places = jnp.stack([jnp.asarray(v).astype(jnp.int32) for v in places])
    facts = [col == q, own_panel, mem * local_rows, (pan * n_mem + mem) * local_rows, col * width, *col_places]
    facts = jnp.stack([jnp.asarray(f).astype(jnp.int32) for f in facts])
    facts, places = lax.optimization_barrier((facts, places))
    high, low, panel_data = panel_step(pieces, plan, places, width, samples_all, samples_all)
    if rest:
        held = lax.optimization_barrier((high, *rest[1:]))
        high = held[0]
        rest = [rest[0], *held[1:]]
        col_pieces = rest + [rest_twin] + [lax.ppermute(v, "col", swap) for v in rest[1:]]
    return tile_step(
        facts, panel_data, high, low, panel_scores, masked, col_pieces, n_places, col_plan, row_plan, extra, samples_all
    )


def solution(mesh):
    n_samp, n_row, n_col = (mesh.shape[a] for a in ("samp", "row", "col"))
    inner = Mesh(mesh.devices.reshape(n_samp, n_col, n_row // n_col, n_col), ("samp", "pan", "mem", "col"))
    row = ("pan", "mem")
    return jax.shard_map(
        on_device,
        mesh=inner,
        in_specs=(P("samp", row), P(row), P(None, row), P(row), P()),
        out_specs=(P(row, "col"), P(), P(None, row)),
        check_vma=False,
    )
```

```python
import functools

import jax
import jax.numpy as jnp
from jax import lax
from jax.experimental import pallas as pl
from jax.experimental.pallas import tpu as pltpu
from jax.sharding import Mesh
from jax.sharding import PartitionSpec as P

ridge = 0.1
F32 = jnp.float32
BF16 = jnp.bfloat16
NN = (((1,), (0,)), ((), ()))
NT = (((1,), (1,)), ((), ()))
block = 128
sublanes = 8
panel_vmem = 30 * 2**20
tile_vmem = 36 * 2**20


def dot1(a, b, dims):
    return lax.dot_general(a, b, dims, preferred_element_type=F32)


def split(x):
    high = x.astype(BF16)
    return high, (x - high.astype(F32)).astype(BF16)


def dot3(a, b, dims):
    (along_a,), (along_b,) = dims[0]
    left = jnp.concatenate([a[0], a[0], a[1]], axis=along_a)
    right = jnp.concatenate([b[0], b[1], b[0]], axis=along_b)
    return dot1(left, right, dims)


def row_to_all(v, i):
    return jnp.broadcast_to(v[i : i + 1, :], v.shape)


def lane_to_all(v, j):
    return jnp.take_along_axis(v, jnp.full(v.shape, j, jnp.int32), axis=1)


def take_away(base, coefs, rows):
    t = [c * r for c, r in zip(coefs, rows)]
    return base - (((t[0] + t[1]) + (t[2] + t[3])) + ((t[4] + t[5]) + (t[6] + t[7])))


def inverse_factor(rows, beside=None):
    count = block // sublanes
    sub = lax.broadcasted_iota(jnp.int32, (sublanes, block), 0)
    lane = lax.broadcasted_iota(jnp.int32, (sublanes, block), 1)
    rows = list(rows)
    out = []
    diag = [lane_to_all(rows[0], j) for j in range(sublanes)]
    for p in range(count):
        first = sublanes * p
        inside = (lane >= first) & (lane < first + sublanes)
        work = jnp.where(inside, jnp.where(lane - first == sub, 1.0, 0.0), rows[p])
        near = range(p + 1, min(count, p + (4 if p % 2 == 0 else 3)))
        below = {g: [lane_to_all(rows[g], first + j) for j in range(sublanes)] for g in near}
        more = p + 1 < count
        if more:
            after = [lane_to_all(rows[p + 1], first + sublanes + m) for m in range(sublanes)]
            entry_next = list(below[p + 1])
        scaled = []
        done = jnp.zeros((sublanes, block), F32)
        raw = diag[0]
        for j in range(sublanes):
            pivot = row_to_all(raw, j)
            inv = 1.0 / pivot
            ratio = diag[j] * inv
            here = sub == j
            row = row_to_all(work, j)
            done = jnp.where(here, row * lax.rsqrt(pivot), done)
            work = jnp.where(here, row * inv, work - ratio * row)
            if more:
                scaled.append(entry_next[j] * inv)
            for m in range(j + 1, sublanes):
                entry = row_to_all(diag[m], j)
                left = diag[m] - ratio * entry
                if m == j + 1:
                    raw = left
                diag[m] = jnp.where(here, entry * inv, left)
                if more:
                    entry_next[m] = entry_next[m] - scaled[j] * entry
        out.append(jnp.where(lane <= first + sub, done, 0.0))
        if beside is not None:
            beside(p)
        if more:
            diag = [
                take_away(after[m], scaled, [row_to_all(entry_next[j], m) for j in range(sublanes)])
                for m in range(sublanes)
            ]
        work_rows = [row_to_all(work, j) for j in range(sublanes)]
        for g in near:
            rows[g] = take_away(jnp.where(inside, 0.0, rows[g]), below[g], work_rows)
        if p % 2 == 0:
            before, inside_before = work, inside
            continue
        far = range(p + 3, count)
        if not far:
            continue
        tie = [lane_to_all(before, first + m) for m in range(sublanes)]
        before = take_away(jnp.where(inside, 0.0, before), tie, work_rows)
        pair = split(jnp.concatenate([before, work], axis=0))
        top, bottom = first - sublanes, block - first - sublanes
        pair = tuple(
            jnp.concatenate(
                [jnp.zeros((h, block), BF16) if v is None else v for h, v in ((top, None), (0, w), (bottom, None)) if h or v is not None],
                axis=0,
            )
            for w in pair
        )
        change = dot3(split(jnp.concatenate([rows[g] for g in far], axis=0)), pair, NN)
        for i, g in enumerate(far):
            kept = jnp.where(inside | inside_before, 0.0, rows[g])
            rows[g] = kept - change[sublanes * i : sublanes * (i + 1)]
    return out


def invert_in_place(a, n, corner, fill, high, low, columns, line, finish):
    def factor_of(value, beside=None):
        return split(
            jnp.concatenate(
                inverse_factor([value[sublanes * g : sublanes * (g + 1)] for g in range(block // sublanes)], beside), axis=0
            )
        )

    def make_line(k):
        first = pl.multiple_of(k * block, block)
        here = pl.ds(first, block)
        small = (high[here, here], low[here, here])
        at = lax.broadcasted_iota(jnp.int32, (block, n), 0)
        across = lax.broadcasted_iota(jnp.int32, (block, n), 1) - first
        inside = (across >= 0) & (across < block)
        given = jnp.where(inside, jnp.where(at == across, 1.0, 0.0), a[here, :])
        found = dot3(small, split(given), NN)
        high[here, :], low[here, :] = split(jnp.where(across < block, found, 0.0))
        finish(k)
        return found

    def step(k, carry):
        first = pl.multiple_of(k * block, block)
        after = pl.ds(pl.multiple_of(first + block, block), block)
        here = pl.ds(first, block)
        small = (high[here, here], low[here, here])
        left = split(dot3(split(a[after, here]), small, NT))
        corner = a[after, after] - dot3(left, left, NT)
        across = lax.broadcasted_iota(jnp.int32, (128, n), 1) - first
        inside = (across >= 0) & (across < block)
        turns = [2 * i for i in range(1, n // block)] + [n // block * 2 - 1]

        def beside(p):
            if p == 0:
                line[0], line[1] = split(make_line(k))
            if p == 1:
                columns[0], columns[1] = split(dot3(split(a[:, here]), small, NT))
            if p in turns:
                i0 = turns.index(p) * 128
                i1 = i0 + 128
                change = dot3((columns[0, i0:i1, :], columns[1, i0:i1, :]), (line[0], line[1]), NN)
                a[i0:i1, :] = jnp.where(inside, 0.0, a[i0:i1, :]) - change

        high[after, after], low[after, after] = factor_of(corner, beside)
        return carry

    high[0:block, 0:block], low[0:block, 0:block] = factor_of(corner, fill)
    lax.fori_loop(0, n // block - 1, step, 0)
    make_line(n // block - 1)


def panel_kernel(plan, samples_all, places, *refs):
    count = len(plan)
    pieces, (high_ref, low_ref, panel_ref, data, a, high, low, columns, line, in_sem, out_sem) = refs[:count], refs[count:]
    width, samples = data.shape
    copies = []
    for i, (piece, slots) in enumerate(zip(pieces, plan)):
        tall, depth = piece.shape[1:]
        place = pl.multiple_of(places[i], block)
        for t, slot in enumerate(slots):
            at = pl.multiple_of(places[count + slot] * depth, block)
            copies.append(
                pltpu.make_async_copy(piece.at[t], data.at[pl.ds(place, tall), pl.ds(at, depth)], in_sem)
            )
    for c in copies:
        c.start()
    for c in copies:
        c.wait()
    keep = pltpu.make_async_copy(data, panel_ref, out_sem)
    keep.start()
    step = 2 * block

    def linkage_rows(i0, tall, wide):
        part = dot1(data[i0 : i0 + tall, :], data[0:wide, :], NT) / samples_all
        at = lax.broadcasted_iota(jnp.int32, part.shape, 0) + i0
        across = lax.broadcasted_iota(jnp.int32, part.shape, 1)
        return part + jnp.where(at == across, ridge, 0.0)

    def fill(p):
        turns = block // sublanes * step // width
        if p % turns == 0:
            i0 = p // turns * step
            a[i0 : i0 + step, :] = linkage_rows(i0, step, width)

    def out_copies(k):
        here = pl.ds(pl.multiple_of(k * block, block), block)
        return [
            pltpu.make_async_copy(source.at[here, :], target.at[here, :], out_sem)
            for source, target in ((high, high_ref), (low, low_ref))
        ]

    def finish(k):
        for c in out_copies(k):
            c.start()

    invert_in_place(a, width, linkage_rows(0, block, block), fill, high, low, columns, line, finish)
    for k in range(width // block):
        for c in out_copies(k):
            c.wait()
    keep.wait()


def panel_step(pieces, plan, places, width, samples, samples_all):
    return pl.pallas_call(
        functools.partial(panel_kernel, plan, samples_all),
        out_shape=(
            jax.ShapeDtypeStruct((width, width), BF16),
            jax.ShapeDtypeStruct((width, width), BF16),
            jax.ShapeDtypeStruct((width, samples), BF16),
        ),
        in_specs=[pl.BlockSpec(memory_space=pltpu.SMEM)] + [pl.BlockSpec(memory_space=pl.ANY)] * len(pieces),
        out_specs=(pl.BlockSpec(memory_space=pl.ANY),) * 3,
        scratch_shapes=[
            pltpu.VMEM((width, samples), BF16),
            pltpu.VMEM((width, width), F32),
            pltpu.VMEM((width, width), BF16),
            pltpu.VMEM((width, width), BF16),
            pltpu.VMEM((2, width, block), BF16),
            pltpu.VMEM((2, block, width), BF16),
            pltpu.SemaphoreType.DMA,
            pltpu.SemaphoreType.DMA,
        ],
        compiler_params=pltpu.CompilerParams(vmem_limit_bytes=panel_vmem),
        cost_estimate=pl.CostEstimate(flops=40 * 10**9, bytes_accessed=20 * 2**20, transcendentals=0),
    )(places, *pieces)


def tile_kernel(samples_all, n_places, n_scores, col_plan, row_plan, facts, panel_ref, high_ref, low_ref, own_ref, *refs):
    score_refs, refs = refs[:n_scores], refs[n_scores:]
    pieces = refs[: len(col_plan)]
    cond_ref, whitened_ref, residual_ref, panel, cols, rows, high, low, change, sems = refs[-10:]
    extra = refs[len(col_plan) : -10]
    width, samples = panel.shape
    local_rows = rows.shape[0]
    row_place_panel = pl.multiple_of(facts[2], block)
    n_facts, slot_at = 5, 5 + n_places
    cols_own, rows_own = facts[0] == 1, facts[1] == 1
    load_panel = pltpu.make_async_copy(panel_ref, panel, sems.at[0])

    def copies(piece, target, first, plan, sem):
        tall, depth = piece.shape[1:]
        found = []
        for t, place, slot in plan:
            at = pl.multiple_of((facts[n_facts + place] if place >= 0 else 0) - first, block)
            across = pl.multiple_of(facts[slot_at + slot] * depth, block)
            found.append(
                pltpu.make_async_copy(piece.at[t], target.at[pl.ds(at, tall), pl.ds(across, depth)], sem)
            )
        return found

    def col_copies():
        return [c for p, plan in zip(pieces, col_plan) for c in copies(p, cols, 0, plan, sems.at[1])]

    def row_copies():
        if extra:
            return copies(extra[0], rows, 0, row_plan[0], sems.at[2])
        return [c for p, plan in zip(pieces, row_plan) for c in copies(p, rows, facts[2], plan, sems.at[2])]

    cols_from_panel = pltpu.make_async_copy(panel_ref, cols, sems.at[1])
    rows_from_panel = pltpu.make_async_copy(
        panel_ref.at[pl.ds(row_place_panel, local_rows), :], rows, sems.at[2]
    )

    @pl.when(rows_own)
    def _():
        rows_from_panel.start()

    @pl.when(jnp.logical_not(rows_own))
    def _():
        for c in row_copies():
            c.start()

    load_panel.start()
    loads = [
        pltpu.make_async_copy(source, target, sems.at[3]) for source, target in ((high_ref, high), (low_ref, low))
    ]
    for c in loads:
        c.start()
    @pl.when(cols_own)
    def _():
        cols_from_panel.start()

    @pl.when(jnp.logical_not(cols_own))
    def _():
        for c in col_copies():
            c.start()

    inverse = (high, low)
    step = 2 * block
    load_panel.wait()

    @pl.when(rows_own)
    def _():
        rows_from_panel.wait()

    @pl.when(jnp.logical_not(rows_own))
    def _():
        for c in row_copies():
            c.wait()

    tall = min(256, local_rows)
    chunks = [(r0, r0 + tall) for r0 in range(0, local_rows, tall)]
    tiles = [(j0, j0 + step) for j0 in range(0, width, step)]
    slabs = []
    for r0, r1 in chunks:
        slab = dot1(rows[r0:r1, :], panel[...], NT) / samples_all
        at = lax.broadcasted_iota(jnp.int32, slab.shape, 0) + (row_place_panel + r0)
        across = lax.broadcasted_iota(jnp.int32, slab.shape, 1)
        slabs.append(split(slab + jnp.where((at == across) & rows_own, ridge, 0.0)))
    for c in loads:
        c.wait()
    factors = []
    for slab in slabs:
        parts = [
            dot3(tuple(v[:, :j1] for v in slab), tuple(v[j0:j1, :j1] for v in inverse), NT) for j0, j1 in tiles
        ]
        factors.append(split(jnp.concatenate(parts, axis=1)))
    weights = []
    for (r0, r1), factor in zip(chunks, factors):
        parts = [
            dot3(tuple(v[:, j0:] for v in factor), tuple(v[j0:, j0:j1] for v in inverse), NN) for j0, j1 in tiles
        ]
        value = jnp.concatenate(parts, axis=1)
        cond_ref[r0:r1, :] = value
        weights.append(split(value))
    scores = score_refs[0][...]
    if n_scores == 2:
        beside = score_refs[1][...]
        first = row_place_panel == 0
        scores = jnp.concatenate([jnp.where(first, scores, beside), jnp.where(first, beside, scores)], axis=1)
    scores = split(scores)
    for j0, j1 in tiles:
        whitened_ref[:, j0:j1] = dot3(
            tuple(v[:, :j1] for v in scores), tuple(v[j0:j1, :j1] for v in inverse), NT
        )
    for (r0, r1), parts in zip(chunks, weights):
        both = jnp.concatenate([panel[...], panel[...]], axis=0)
        explained = dot1(jnp.concatenate(parts, axis=1), both, NN)
        change[r0:r1, :] = (rows[r0:r1, :].astype(F32) - explained).astype(BF16)
    whitened = split(whitened_ref[...])
    for (r0, r1), factor in zip(chunks, factors):
        residual_ref[:, r0:r1] = own_ref[:, r0:r1] - dot3(whitened, factor, NT)

    @pl.when(cols_own)
    def _():
        cols_from_panel.wait()

    @pl.when(jnp.logical_not(cols_own))
    def _():
        for c in col_copies():
            c.wait()

    row_first, col_first = facts[3], facts[4]
    for r0, r1 in chunks:
        part = dot1(change[r0:r1, :], cols[...], NT) / samples_all
        at = lax.broadcasted_iota(jnp.int32, part.shape, 0) + (row_first + r0)
        across = lax.broadcasted_iota(jnp.int32, part.shape, 1) + col_first
        unit = jnp.where(at == across, 1.0, 0.0)
        cond_ref[r0:r1, :] = part + ridge * (unit - jnp.where(cols_own, cond_ref[r0:r1, :], 0.0))


def tile_step(facts, panel, high, low, scores, own, pieces, n_places, col_plan, row_plan, extra, samples_all):
    width, samples = panel.shape
    traits, local_rows = own.shape
    smem = pl.BlockSpec(memory_space=pltpu.SMEM)
    vmem = pl.BlockSpec(memory_space=pltpu.VMEM)
    anywhere = pl.BlockSpec(memory_space=pl.ANY)
    return pl.pallas_call(
        functools.partial(tile_kernel, samples_all, n_places, len(scores), col_plan, row_plan),
        out_shape=(
            jax.ShapeDtypeStruct((local_rows, width), F32),
            jax.ShapeDtypeStruct((traits, width), F32),
            jax.ShapeDtypeStruct((traits, local_rows), F32),
        ),
        in_specs=[smem] + [anywhere] * 3 + [vmem] * (1 + len(scores)) + [anywhere] * (len(pieces) + len(extra)),
        out_specs=(vmem, vmem, vmem),
        scratch_shapes=[
            pltpu.VMEM((width, samples), BF16),
            pltpu.VMEM((width, samples), BF16),
            pltpu.VMEM((local_rows, samples), BF16),
            pltpu.VMEM((width, width), BF16),
            pltpu.VMEM((width, width), BF16),
            pltpu.VMEM((local_rows, samples), BF16),
            pltpu.SemaphoreType.DMA((4,)),
        ],
        compiler_params=pltpu.CompilerParams(vmem_limit_bytes=tile_vmem),
        cost_estimate=pl.CostEstimate(flops=20 * 10**9, bytes_accessed=20 * 2**20, transcendentals=0),
    )(facts, panel, high, low, own, *scores, *pieces, *extra)


swap = [(0, 1), (1, 0)]


def numbers(values):
    return jnp.stack([jnp.asarray(v).astype(jnp.int32) for v in values])


def on_device(genotypes, frequencies, trait_scores, typed_mask, panel_index):
    n_samp, n_pan, n_mem, n_col = (lax.axis_size(a) for a in ("samp", "pan", "mem", "col"))
    samp, pan, mem, col = (lax.axis_index(a) for a in ("samp", "pan", "mem", "col"))
    depth, local_rows = genotypes.shape
    width = local_rows * n_mem
    samples_all = depth * n_samp
    q = panel_index[0] % n_col
    spread = jnp.sqrt(2.0 * frequencies * (1.0 - frequencies))
    standard = ((genotypes.astype(F32) - 2.0 * frequencies) / spread).astype(BF16).T
    masked = trait_scores * typed_mask.astype(F32)
    own_panel = pan == q
    rest = []
    common = [col == q, own_panel, mem * local_rows, (pan * n_mem + mem) * local_rows, col * width]
    if n_pan == 2 and n_mem == 2 and n_col == 2 and n_samp == 4:
        quarter = local_rows // 4

        def part(i, j):
            return lax.dynamic_slice_in_dim(standard, (2 * i + j) * quarter, quarter, 0)

        mine, other = part(pan, col), lax.ppermute(part(1 - pan, col), "pan", swap)
        piece = jnp.where(own_panel, mine, other)
        rest_piece = jnp.where(own_panel, other, mine)

        def along_samp(v):
            steps = [[(s, (s + d) % n_samp) for s in range(n_samp)] for d in (1, 2, 3)]
            return [lax.ppermute(v, "samp", pairs) for pairs in steps]

        own = jnp.stack([piece] + along_samp(piece))
        panel_masked = jnp.where(own_panel, masked, lax.ppermute(masked, "pan", swap))
        corners = ((mem, pan), (1 - mem, pan), (mem, 1 - pan), (1 - mem, 1 - pan))
        slots = [(samp - d) % n_samp for d in range(n_samp)]

        def place(m, a, c):
            return (m * 4 + a * 2 + c) * quarter

        places = numbers([place(m, a, c) for c in (col, 1 - col) for m, a in corners + corners[3:]] + slots)
        facts = numbers(common + [place(m, a, c) for c in (col, 1 - col) for m, a in corners] + slots)
        own, panel_masked, places, facts = lax.optimization_barrier((own, panel_masked, places, facts))
        beside = lax.ppermute(panel_masked, "mem", swap)
        by_mem, by_pan = lax.ppermute(own, "mem", swap), lax.ppermute(own, "pan", swap)
        far_a = lax.ppermute(by_pan[:2], "mem", swap)
        far_b = lax.ppermute(by_mem[2:], "pan", swap)
        near = [own, by_mem, by_pan, far_a, far_b]
        twin = [lax.ppermute(v, "col", swap) for v in near]
        pieces = near + twin
        plan = [(0, 1, 2, 3)] * 3 + [(0, 1), (2, 3)]
        plan = plan + plan
        rest_piece, _ = lax.optimization_barrier((rest_piece, own))
        rest_own = jnp.stack([rest_piece] + along_samp(rest_piece))
        rest_own, _, _, beside = lax.optimization_barrier((rest_own, by_mem, by_pan, beside))
        cross = [(2 * i + j, 2 * (1 - i) + 1 - j) for i in range(2) for j in range(2)]
        rest = [
            rest_own,
            lax.ppermute(rest_own, "mem", swap),
            lax.ppermute(rest_own, "pan", swap),
            lax.ppermute(rest_own, ("pan", "mem"), cross),
        ]
        rest_twin = lax.ppermute(rest_own, "col", swap)
        col_plan = [[(d, t + 4 * c, d) for d in range(4)] for c in range(2) for t in range(4)]
        row_plan = [plan if i % 2 == 0 else [] for i, plan in enumerate(col_plan)]
        extra, n_places = [], 8
        panel_scores = [panel_masked, beside]
    else:
        chosen = lax.psum(jnp.where(own_panel, standard, jnp.zeros_like(standard)), "pan")
        gathered = lax.all_gather(chosen, ("samp", "mem")).reshape(n_samp, width, depth)
        pieces, plan = [gathered], [tuple(range(n_samp))]
        places = [0, *range(n_samp)]
        cross = [(i * n_col + j, j * n_col + i) for i in range(n_pan) for j in range(n_col)]
        col_block = lax.ppermute(standard, ("pan", "col"), cross)
        col_pieces = [lax.all_gather(col_block, ("samp", "mem")).reshape(n_samp, width, depth)]
        extra, n_places = [lax.all_gather(standard, "samp")], 1
        col_plan = [[(s, 0, s) for s in range(n_samp)]]
        row_plan = [[(s, -1, s) for s in range(n_samp)]]
        facts = numbers(common + places)
        places = numbers(places)
        panel_masked = lax.psum(jnp.where(own_panel, masked, jnp.zeros_like(masked)), "pan")
        panel_scores = [lax.all_gather(panel_masked, "mem", axis=1, tiled=True)]
    high, low, panel_data = panel_step(pieces, plan, places, width, samples_all, samples_all)
    if rest:
        held = lax.optimization_barrier((high, *rest[1:]))
        high = held[0]
        rest = [rest[0], *held[1:]]
        col_pieces = rest + [rest_twin] + [lax.ppermute(v, "col", swap) for v in rest[1:]]
    return tile_step(
        facts, panel_data, high, low, panel_scores, masked, col_pieces, n_places, col_plan, row_plan, extra, samples_all
    )


def solution(mesh):
    n_samp, n_row, n_col = (mesh.shape[a] for a in ("samp", "row", "col"))
    inner = Mesh(mesh.devices.reshape(n_samp, n_col, n_row // n_col, n_col), ("samp", "pan", "mem", "col"))
    row = ("pan", "mem")
    return jax.shard_map(
        on_device,
        mesh=inner,
        in_specs=(P("samp", row), P(row), P(None, row), P(row), P()),
        out_specs=(P(row, "col"), P(), P(None, row)),
        check_vma=False,
    )
```

```python
import functools

import jax
import jax.numpy as jnp
from jax import lax
from jax.experimental import pallas as pl
from jax.experimental.pallas import tpu as pltpu
from jax.sharding import Mesh
from jax.sharding import PartitionSpec as P

ridge = 0.1
F32 = jnp.float32
BF16 = jnp.bfloat16
NN = (((1,), (0,)), ((), ()))
NT = (((1,), (1,)), ((), ()))
block = 128
sublanes = 8
panel_vmem = 30 * 2**20
tile_vmem = 36 * 2**20


def dot1(a, b, dims):
    return lax.dot_general(a, b, dims, preferred_element_type=F32)


def split(x):
    high = x.astype(BF16)
    return high, (x - high.astype(F32)).astype(BF16)


def dot3(a, b, dims):
    (along_a,), (along_b,) = dims[0]
    left = jnp.concatenate([a[0], a[0], a[1]], axis=along_a)
    right = jnp.concatenate([b[0], b[1], b[0]], axis=along_b)
    return dot1(left, right, dims)


def row_to_all(v, i):
    return jnp.broadcast_to(v[i : i + 1, :], v.shape)


def lane_to_all(v, j):
    return jnp.take_along_axis(v, jnp.full(v.shape, j, jnp.int32), axis=1)


def take_away(base, coefs, rows):
    t = [c * r for c, r in zip(coefs, rows)]
    return base - (((t[0] + t[1]) + (t[2] + t[3])) + ((t[4] + t[5]) + (t[6] + t[7])))


def inverse_factor(rows, beside=None):
    count = block // sublanes
    sub = lax.broadcasted_iota(jnp.int32, (sublanes, block), 0)
    lane = lax.broadcasted_iota(jnp.int32, (sublanes, block), 1)
    rows = list(rows)
    out = []
    diag = [lane_to_all(rows[0], j) for j in range(sublanes)]
    for p in range(count):
        first = sublanes * p
        inside = (lane >= first) & (lane < first + sublanes)
        work = jnp.where(inside, jnp.where(lane - first == sub, 1.0, 0.0), rows[p])
        near = range(p + 1, min(count, p + (4 if p % 2 == 0 else 3)))
        below = {g: [lane_to_all(rows[g], first + j) for j in range(sublanes)] for g in near}
        more = p + 1 < count
        if more:
            after = [lane_to_all(rows[p + 1], first + sublanes + m) for m in range(sublanes)]
            entry_next = list(below[p + 1])
        scaled = []
        done = jnp.zeros((sublanes, block), F32)
        raw = diag[0]
        for j in range(sublanes):
            pivot = row_to_all(raw, j)
            inv = 1.0 / pivot
            ratio = diag[j] * inv
            here = sub == j
            row = row_to_all(work, j)
            done = jnp.where(here, row * lax.rsqrt(pivot), done)
            work = jnp.where(here, row * inv, work - ratio * row)
            if more:
                scaled.append(entry_next[j] * inv)
            for m in range(j + 1, sublanes):
                entry = row_to_all(diag[m], j)
                left = diag[m] - ratio * entry
                if m == j + 1:
                    raw = left
                diag[m] = jnp.where(here, entry * inv, left)
                if more:
                    entry_next[m] = entry_next[m] - scaled[j] * entry
        out.append(jnp.where(lane <= first + sub, done, 0.0))
        if beside is not None:
            beside(p)
        if more:
            diag = [
                take_away(after[m], scaled, [row_to_all(entry_next[j], m) for j in range(sublanes)])
                for m in range(sublanes)
            ]
        work_rows = [row_to_all(work, j) for j in range(sublanes)]
        for g in near:
            rows[g] = take_away(jnp.where(inside, 0.0, rows[g]), below[g], work_rows)
        if p % 2 == 0:
            before, inside_before = work, inside
            continue
        far = range(p + 3, count)
        if not far:
            continue
        tie = [lane_to_all(before, first + m) for m in range(sublanes)]
        before = take_away(jnp.where(inside, 0.0, before), tie, work_rows)
        pair = split(jnp.concatenate([before, work], axis=0))
        top, bottom = first - sublanes, block - first - sublanes
        pair = tuple(
            jnp.concatenate(
                [jnp.zeros((h, block), BF16) if v is None else v for h, v in ((top, None), (0, w), (bottom, None)) if h or v is not None],
                axis=0,
            )
            for w in pair
        )
        change = dot3(split(jnp.concatenate([rows[g] for g in far], axis=0)), pair, NN)
        for i, g in enumerate(far):
            kept = jnp.where(inside | inside_before, 0.0, rows[g])
            rows[g] = kept - change[sublanes * i : sublanes * (i + 1)]
    return out


def invert_in_place(a, n, corner, fill, high, low, columns, line, finish):
    def factor_of(value, beside=None):
        return split(
            jnp.concatenate(
                inverse_factor([value[sublanes * g : sublanes * (g + 1)] for g in range(block // sublanes)], beside), axis=0
            )
        )

    def make_line(k):
        first = pl.multiple_of(k * block, block)
        here = pl.ds(first, block)
        small = (high[here, here], low[here, here])
        at = lax.broadcasted_iota(jnp.int32, (block, n), 0)
        across = lax.broadcasted_iota(jnp.int32, (block, n), 1) - first
        inside = (across >= 0) & (across < block)
        given = jnp.where(inside, jnp.where(at == across, 1.0, 0.0), a[here, :])
        found = dot3(small, split(given), NN)
        high[here, :], low[here, :] = split(jnp.where(across < block, found, 0.0))
        finish(k)
        return found

    def step(k, carry):
        first = pl.multiple_of(k * block, block)
        after = pl.ds(pl.multiple_of(first + block, block), block)
        here = pl.ds(first, block)
        small = (high[here, here], low[here, here])
        left = split(dot3(split(a[after, here]), small, NT))
        corner = a[after, after] - dot3(left, left, NT)
        across = lax.broadcasted_iota(jnp.int32, (128, n), 1) - first
        inside = (across >= 0) & (across < block)
        turns = [2 * i for i in range(1, n // block)] + [n // block * 2 - 1]

        def beside(p):
            if p == 0:
                line[0], line[1] = split(make_line(k))
            if p == 1:
                columns[0], columns[1] = split(dot3(split(a[:, here]), small, NT))
            if p in turns:
                i0 = turns.index(p) * 128
                i1 = i0 + 128
                change = dot3((columns[0, i0:i1, :], columns[1, i0:i1, :]), (line[0], line[1]), NN)
                a[i0:i1, :] = jnp.where(inside, 0.0, a[i0:i1, :]) - change

        high[after, after], low[after, after] = factor_of(corner, beside)
        return carry

    high[0:block, 0:block], low[0:block, 0:block] = factor_of(corner, fill)
    lax.fori_loop(0, n // block - 1, step, 0)
    make_line(n // block - 1)


def panel_kernel(plan, samples_all, places, *refs):
    count = len(plan)
    pieces, (high_ref, low_ref, panel_ref, data, a, high, low, columns, line, in_sem, out_sem) = refs[:count], refs[count:]
    width, samples = data.shape
    copies = []
    for i, (piece, slots) in enumerate(zip(pieces, plan)):
        tall, depth = piece.shape[1:]
        place = pl.multiple_of(places[i], block)
        for t, slot in enumerate(slots):
            at = pl.multiple_of(places[count + slot] * depth, block)
            copies.append(
                pltpu.make_async_copy(piece.at[t], data.at[pl.ds(place, tall), pl.ds(at, depth)], in_sem)
            )
    for c in copies:
        c.start()
    for c in copies:
        c.wait()
    keep = pltpu.make_async_copy(data, panel_ref, out_sem)
    keep.start()
    step = 2 * block

    def linkage_rows(i0, tall, wide):
        part = dot1(data[i0 : i0 + tall, :], data[0:wide, :], NT) / samples_all
        at = lax.broadcasted_iota(jnp.int32, part.shape, 0) + i0
        across = lax.broadcasted_iota(jnp.int32, part.shape, 1)
        return part + jnp.where(at == across, ridge, 0.0)

    def fill(p):
        turns = block // sublanes * step // width
        if p % turns == 0:
            i0 = p // turns * step
            a[i0 : i0 + step, :] = linkage_rows(i0, step, width)

    def out_copies(k):
        here = pl.ds(pl.multiple_of(k * block, block), block)
        return [
            pltpu.make_async_copy(source.at[here, :], target.at[here, :], out_sem)
            for source, target in ((high, high_ref), (low, low_ref))
        ]

    def finish(k):
        for c in out_copies(k):
            c.start()

    invert_in_place(a, width, linkage_rows(0, block, block), fill, high, low, columns, line, finish)
    for k in range(width // block):
        for c in out_copies(k):
            c.wait()
    keep.wait()


def panel_step(pieces, plan, places, width, samples, samples_all):
    return pl.pallas_call(
        functools.partial(panel_kernel, plan, samples_all),
        out_shape=(
            jax.ShapeDtypeStruct((width, width), BF16),
            jax.ShapeDtypeStruct((width, width), BF16),
            jax.ShapeDtypeStruct((width, samples), BF16),
        ),
        in_specs=[pl.BlockSpec(memory_space=pltpu.SMEM)] + [pl.BlockSpec(memory_space=pl.ANY)] * len(pieces),
        out_specs=(pl.BlockSpec(memory_space=pl.ANY),) * 3,
        scratch_shapes=[
            pltpu.VMEM((width, samples), BF16),
            pltpu.VMEM((width, width), F32),
            pltpu.VMEM((width, width), BF16),
            pltpu.VMEM((width, width), BF16),
            pltpu.VMEM((2, width, block), BF16),
            pltpu.VMEM((2, block, width), BF16),
            pltpu.SemaphoreType.DMA,
            pltpu.SemaphoreType.DMA,
        ],
        compiler_params=pltpu.CompilerParams(vmem_limit_bytes=panel_vmem),
        cost_estimate=pl.CostEstimate(flops=40 * 10**9, bytes_accessed=20 * 2**20, transcendentals=0),
    )(places, *pieces)


def tile_kernel(samples_all, n_places, n_scores, col_plan, row_plan, facts, panel_ref, high_ref, low_ref, own_ref, *refs):
    score_refs, refs = refs[:n_scores], refs[n_scores:]
    pieces = refs[: len(col_plan)]
    cond_ref, whitened_ref, residual_ref, panel, cols, rows, high, low, change, sems = refs[-10:]
    extra = refs[len(col_plan) : -10]
    width, samples = panel.shape
    local_rows = rows.shape[0]
    row_place_panel = pl.multiple_of(facts[2], block)
    n_facts, slot_at = 5, 5 + n_places
    cols_own, rows_own = facts[0] == 1, facts[1] == 1
    load_panel = pltpu.make_async_copy(panel_ref, panel, sems.at[0])

    def copies(piece, target, first, plan, sem):
        tall, depth = piece.shape[1:]
        found = []
        for t, place, slot in plan:
            at = pl.multiple_of((facts[n_facts + place] if place >= 0 else 0) - first, block)
            across = pl.multiple_of(facts[slot_at + slot] * depth, block)
            found.append(
                pltpu.make_async_copy(piece.at[t], target.at[pl.ds(at, tall), pl.ds(across, depth)], sem)
            )
        return found

    def col_copies():
        return [c for p, plan in zip(pieces, col_plan) for c in copies(p, cols, 0, plan, sems.at[1])]

    def row_copies():
        if extra:
            return copies(extra[0], rows, 0, row_plan[0], sems.at[2])
        return [c for p, plan in zip(pieces, row_plan) for c in copies(p, rows, facts[2], plan, sems.at[2])]

    cols_from_panel = pltpu.make_async_copy(panel_ref, cols, sems.at[1])
    rows_from_panel = pltpu.make_async_copy(
        panel_ref.at[pl.ds(row_place_panel, local_rows), :], rows, sems.at[2]
    )

    @pl.when(rows_own)
    def _():
        rows_from_panel.start()

    @pl.when(jnp.logical_not(rows_own))
    def _():
        for c in row_copies():
            c.start()

    load_panel.start()
    loads = [
        pltpu.make_async_copy(source, target, sems.at[3]) for source, target in ((high_ref, high), (low_ref, low))
    ]
    for c in loads:
        c.start()
    @pl.when(cols_own)
    def _():
        cols_from_panel.start()

    @pl.when(jnp.logical_not(cols_own))
    def _():
        for c in col_copies():
            c.start()

    inverse = (high, low)
    step = 2 * block
    load_panel.wait()

    @pl.when(rows_own)
    def _():
        rows_from_panel.wait()

    @pl.when(jnp.logical_not(rows_own))
    def _():
        for c in row_copies():
            c.wait()

    tall = min(256, local_rows)
    chunks = [(r0, r0 + tall) for r0 in range(0, local_rows, tall)]
    tiles = [(j0, j0 + step) for j0 in range(0, width, step)]
    slabs = []
    for r0, r1 in chunks:
        slab = dot1(rows[r0:r1, :], panel[...], NT) / samples_all
        at = lax.broadcasted_iota(jnp.int32, slab.shape, 0) + (row_place_panel + r0)
        across = lax.broadcasted_iota(jnp.int32, slab.shape, 1)
        slabs.append(split(slab + jnp.where((at == across) & rows_own, ridge, 0.0)))
    for c in loads:
        c.wait()
    factors = []
    for slab in slabs:
        parts = [
            dot3(tuple(v[:, :j1] for v in slab), tuple(v[j0:j1, :j1] for v in inverse), NT) for j0, j1 in tiles
        ]
        factors.append(split(jnp.concatenate(parts, axis=1)))
    weights = []
    for (r0, r1), factor in zip(chunks, factors):
        parts = [
            dot3(tuple(v[:, j0:] for v in factor), tuple(v[j0:, j0:j1] for v in inverse), NN) for j0, j1 in tiles
        ]
        value = jnp.concatenate(parts, axis=1)
        cond_ref[r0:r1, :] = value
        weights.append(split(value))
    scores = score_refs[0][...]
    if n_scores == 2:
        beside = score_refs[1][...]
        first = row_place_panel == 0
        scores = jnp.concatenate([jnp.where(first, scores, beside), jnp.where(first, beside, scores)], axis=1)
    scores = split(scores)
    for j0, j1 in tiles:
        whitened_ref[:, j0:j1] = dot3(
            tuple(v[:, :j1] for v in scores), tuple(v[j0:j1, :j1] for v in inverse), NT
        )
    for (r0, r1), parts in zip(chunks, weights):
        both = jnp.concatenate([panel[...], panel[...]], axis=0)
        explained = dot1(jnp.concatenate(parts, axis=1), both, NN)
        change[r0:r1, :] = (rows[r0:r1, :].astype(F32) - explained).astype(BF16)
    whitened = split(whitened_ref[...])
    for (r0, r1), factor in zip(chunks, factors):
        residual_ref[:, r0:r1] = own_ref[:, r0:r1] - dot3(whitened, factor, NT)

    @pl.when(cols_own)
    def _():
        cols_from_panel.wait()

    @pl.when(jnp.logical_not(cols_own))
    def _():
        for c in col_copies():
            c.wait()

    row_first, col_first = facts[3], facts[4]
    for r0, r1 in chunks:
        part = dot1(change[r0:r1, :], cols[...], NT) / samples_all
        at = lax.broadcasted_iota(jnp.int32, part.shape, 0) + (row_first + r0)
        across = lax.broadcasted_iota(jnp.int32, part.shape, 1) + col_first
        unit = jnp.where(at == across, 1.0, 0.0)
        cond_ref[r0:r1, :] = part + ridge * (unit - jnp.where(cols_own, cond_ref[r0:r1, :], 0.0))


def tile_step(facts, panel, high, low, scores, own, pieces, n_places, col_plan, row_plan, extra, samples_all):
    width, samples = panel.shape
    traits, local_rows = own.shape
    smem = pl.BlockSpec(memory_space=pltpu.SMEM)
    vmem = pl.BlockSpec(memory_space=pltpu.VMEM)
    anywhere = pl.BlockSpec(memory_space=pl.ANY)
    return pl.pallas_call(
        functools.partial(tile_kernel, samples_all, n_places, len(scores), col_plan, row_plan),
        out_shape=(
            jax.ShapeDtypeStruct((local_rows, width), F32),
            jax.ShapeDtypeStruct((traits, width), F32),
            jax.ShapeDtypeStruct((traits, local_rows), F32),
        ),
        in_specs=[smem] + [anywhere] * 3 + [vmem] * (1 + len(scores)) + [anywhere] * (len(pieces) + len(extra)),
        out_specs=(vmem, vmem, vmem),
        scratch_shapes=[
            pltpu.VMEM((width, samples), BF16),
            pltpu.VMEM((width, samples), BF16),
            pltpu.VMEM((local_rows, samples), BF16),
            pltpu.VMEM((width, width), BF16),
            pltpu.VMEM((width, width), BF16),
            pltpu.VMEM((local_rows, samples), BF16),
            pltpu.SemaphoreType.DMA((4,)),
        ],
        compiler_params=pltpu.CompilerParams(vmem_limit_bytes=tile_vmem),
        cost_estimate=pl.CostEstimate(flops=20 * 10**9, bytes_accessed=20 * 2**20, transcendentals=0),
    )(facts, panel, high, low, own, *scores, *pieces, *extra)


swap = [(0, 1), (1, 0)]


def numbers(values):
    return jnp.stack([jnp.asarray(v).astype(jnp.int32) for v in values])


def standardized(genotypes, frequencies):
    spread = jnp.sqrt(2.0 * frequencies * (1.0 - frequencies))
    return ((genotypes.astype(F32) - 2.0 * frequencies) / spread).astype(BF16).T


def on_device(genotypes, frequencies, trait_scores, typed_mask, panel_index):
    n_samp, n_pan, n_mem, n_col = (lax.axis_size(a) for a in ("samp", "pan", "mem", "col"))
    samp, pan, mem, col = (lax.axis_index(a) for a in ("samp", "pan", "mem", "col"))
    depth, local_rows = genotypes.shape
    width = local_rows * n_mem
    samples_all = depth * n_samp
    q = panel_index[0] % n_col
    masked = trait_scores * typed_mask.astype(F32)
    own_panel = pan == q
    rest = []
    common = [col == q, own_panel, mem * local_rows, (pan * n_mem + mem) * local_rows, col * width]
    if n_pan == 2 and n_mem == 2 and n_col == 2 and n_samp == 4:
        quarter = local_rows // 4

        def part(i, j):
            at = (2 * i + j) * quarter
            return standardized(
                lax.dynamic_slice_in_dim(genotypes, at, quarter, 1), lax.dynamic_slice_in_dim(frequencies, at, quarter, 0)
            )

        mine, other = part(pan, col), lax.ppermute(part(1 - pan, col), "pan", swap)
        piece = jnp.where(own_panel, mine, other)
        rest_piece = jnp.where(own_panel, other, mine)

        def along_samp(v):
            steps = [[(s, (s + d) % n_samp) for s in range(n_samp)] for d in (1, 2, 3)]
            return [lax.ppermute(v, "samp", pairs) for pairs in steps]

        own = jnp.stack([piece] + along_samp(piece))
        panel_masked = jnp.where(own_panel, masked, lax.ppermute(masked, "pan", swap))
        corners = ((mem, pan), (1 - mem, pan), (mem, 1 - pan), (1 - mem, 1 - pan))
        slots = [(samp - d) % n_samp for d in range(n_samp)]

        def place(m, a, c):
            return (m * 4 + a * 2 + c) * quarter

        places = numbers([place(m, a, c) for c in (col, 1 - col) for m, a in corners + corners[3:]] + slots)
        facts = numbers(common + [place(m, a, c) for c in (col, 1 - col) for m, a in corners] + slots)
        own, panel_masked, places, facts = lax.optimization_barrier((own, panel_masked, places, facts))
        beside = lax.ppermute(panel_masked, "mem", swap)
        by_mem, by_pan = lax.ppermute(own, "mem", swap), lax.ppermute(own, "pan", swap)
        far_a = lax.ppermute(by_pan[:2], "mem", swap)
        far_b = lax.ppermute(by_mem[2:], "pan", swap)
        near = [own, by_mem, by_pan, far_a, far_b]
        twin = [lax.ppermute(v, "col", swap) for v in near]
        pieces = near + twin
        plan = [(0, 1, 2, 3)] * 3 + [(0, 1), (2, 3)]
        plan = plan + plan
        rest_piece, _ = lax.optimization_barrier((rest_piece, own))
        rest_own = jnp.stack([rest_piece] + along_samp(rest_piece))
        rest_own, _, _, beside = lax.optimization_barrier((rest_own, by_mem, by_pan, beside))
        cross = [(2 * i + j, 2 * (1 - i) + 1 - j) for i in range(2) for j in range(2)]
        rest = [
            rest_own,
            lax.ppermute(rest_own, "mem", swap),
            lax.ppermute(rest_own, "pan", swap),
            lax.ppermute(rest_own, ("pan", "mem"), cross),
        ]
        rest_twin = lax.ppermute(rest_own, "col", swap)
        col_plan = [[(d, t + 4 * c, d) for d in range(4)] for c in range(2) for t in range(4)]
        row_plan = [plan if i % 2 == 0 else [] for i, plan in enumerate(col_plan)]
        extra, n_places = [], 8
        panel_scores = [panel_masked, beside]
    else:
        standard = standardized(genotypes, frequencies)
        chosen = lax.psum(jnp.where(own_panel, standard, jnp.zeros_like(standard)), "pan")
        gathered = lax.all_gather(chosen, ("samp", "mem")).reshape(n_samp, width, depth)
        pieces, plan = [gathered], [tuple(range(n_samp))]
        places = [0, *range(n_samp)]
        cross = [(i * n_col + j, j * n_col + i) for i in range(n_pan) for j in range(n_col)]
        col_block = lax.ppermute(standard, ("pan", "col"), cross)
        col_pieces = [lax.all_gather(col_block, ("samp", "mem")).reshape(n_samp, width, depth)]
        extra, n_places = [lax.all_gather(standard, "samp")], 1
        col_plan = [[(s, 0, s) for s in range(n_samp)]]
        row_plan = [[(s, -1, s) for s in range(n_samp)]]
        facts = numbers(common + places)
        places = numbers(places)
        panel_masked = lax.psum(jnp.where(own_panel, masked, jnp.zeros_like(masked)), "pan")
        panel_scores = [lax.all_gather(panel_masked, "mem", axis=1, tiled=True)]
    high, low, panel_data = panel_step(pieces, plan, places, width, samples_all, samples_all)
    if rest:
        held = lax.optimization_barrier((high, *rest[1:]))
        high = held[0]
        rest = [rest[0], *held[1:]]
        col_pieces = rest + [rest_twin] + [lax.ppermute(v, "col", swap) for v in rest[1:]]
    return tile_step(
        facts, panel_data, high, low, panel_scores, masked, col_pieces, n_places, col_plan, row_plan, extra, samples_all
    )


def solution(mesh):
    n_samp, n_row, n_col = (mesh.shape[a] for a in ("samp", "row", "col"))
    inner = Mesh(mesh.devices.reshape(n_samp, n_col, n_row // n_col, n_col), ("samp", "pan", "mem", "col"))
    row = ("pan", "mem")
    return jax.shard_map(
        on_device,
        mesh=inner,
        in_specs=(P("samp", row), P(row), P(None, row), P(row), P()),
        out_specs=(P(row, "col"), P(), P(None, row)),
        check_vma=False,
    )
```

```python
import functools

import jax
import jax.numpy as jnp
from jax import lax
from jax.experimental import pallas as pl
from jax.experimental.pallas import tpu as pltpu
from jax.sharding import Mesh
from jax.sharding import PartitionSpec as P

ridge = 0.1
F32 = jnp.float32
BF16 = jnp.bfloat16
NN = (((1,), (0,)), ((), ()))
NT = (((1,), (1,)), ((), ()))
block = 128
sublanes = 8
panel_vmem = 30 * 2**20
tile_vmem = 36 * 2**20


def dot1(a, b, dims):
    return lax.dot_general(a, b, dims, preferred_element_type=F32)


def split(x):
    high = x.astype(BF16)
    return high, (x - high.astype(F32)).astype(BF16)


def dot3(a, b, dims):
    (along_a,), (along_b,) = dims[0]
    left = jnp.concatenate([a[0], a[0], a[1]], axis=along_a)
    right = jnp.concatenate([b[0], b[1], b[0]], axis=along_b)
    return dot1(left, right, dims)


def row_to_all(v, i):
    return jnp.broadcast_to(v[i : i + 1, :], v.shape)


def lane_to_all(v, j):
    return jnp.take_along_axis(v, jnp.full(v.shape, j, jnp.int32), axis=1)


def take_away(base, coefs, rows):
    t = [c * r for c, r in zip(coefs, rows)]
    return base - (((t[0] + t[1]) + (t[2] + t[3])) + ((t[4] + t[5]) + (t[6] + t[7])))


def inverse_factor(rows, beside=None):
    count = block // sublanes
    sub = lax.broadcasted_iota(jnp.int32, (sublanes, block), 0)
    lane = lax.broadcasted_iota(jnp.int32, (sublanes, block), 1)
    rows = list(rows)
    out = []
    diag = [lane_to_all(rows[0], j) for j in range(sublanes)]
    for p in range(count):
        first = sublanes * p
        inside = (lane >= first) & (lane < first + sublanes)
        work = jnp.where(inside, jnp.where(lane - first == sub, 1.0, 0.0), rows[p])
        near = range(p + 1, min(count, p + (4 if p % 2 == 0 else 3)))
        below = {g: [lane_to_all(rows[g], first + j) for j in range(sublanes)] for g in near}
        more = p + 1 < count
        if more:
            after = [lane_to_all(rows[p + 1], first + sublanes + m) for m in range(sublanes)]
            entry_next = list(below[p + 1])
        scaled = []
        done = jnp.zeros((sublanes, block), F32)
        raw = diag[0]
        for j in range(sublanes):
            pivot = row_to_all(raw, j)
            inv = 1.0 / pivot
            ratio = diag[j] * inv
            here = sub == j
            row = row_to_all(work, j)
            done = jnp.where(here, row * lax.rsqrt(pivot), done)
            work = jnp.where(here, row * inv, work - ratio * row)
            if more:
                scaled.append(entry_next[j] * inv)
            for m in range(j + 1, sublanes):
                entry = row_to_all(diag[m], j)
                left = diag[m] - ratio * entry
                if m == j + 1:
                    raw = left
                diag[m] = jnp.where(here, entry * inv, left)
                if more:
                    entry_next[m] = entry_next[m] - scaled[j] * entry
        out.append(jnp.where(lane <= first + sub, done, 0.0))
        if beside is not None:
            beside(p)
        if more:
            diag = [
                take_away(after[m], scaled, [row_to_all(entry_next[j], m) for j in range(sublanes)])
                for m in range(sublanes)
            ]
        work_rows = [row_to_all(work, j) for j in range(sublanes)]
        for g in near:
            rows[g] = take_away(jnp.where(inside, 0.0, rows[g]), below[g], work_rows)
        if p % 2 == 0:
            before, inside_before = work, inside
            continue
        far = range(p + 3, count)
        if not far:
            continue
        tie = [lane_to_all(before, first + m) for m in range(sublanes)]
        before = take_away(jnp.where(inside, 0.0, before), tie, work_rows)
        pair = split(jnp.concatenate([before, work], axis=0))
        top, bottom = first - sublanes, block - first - sublanes
        pair = tuple(
            jnp.concatenate(
                [jnp.zeros((h, block), BF16) if v is None else v for h, v in ((top, None), (0, w), (bottom, None)) if h or v is not None],
                axis=0,
            )
            for w in pair
        )
        change = dot3(split(jnp.concatenate([rows[g] for g in far], axis=0)), pair, NN)
        for i, g in enumerate(far):
            kept = jnp.where(inside | inside_before, 0.0, rows[g])
            rows[g] = kept - change[sublanes * i : sublanes * (i + 1)]
    return out


def invert_in_place(a, n, corner, fill, high, low, columns, line, finish):
    def factor_of(value, beside=None):
        return split(
            jnp.concatenate(
                inverse_factor([value[sublanes * g : sublanes * (g + 1)] for g in range(block // sublanes)], beside), axis=0
            )
        )

    def make_line(k):
        first = pl.multiple_of(k * block, block)
        here = pl.ds(first, block)
        small = (high[here, here], low[here, here])
        at = lax.broadcasted_iota(jnp.int32, (block, n), 0)
        across = lax.broadcasted_iota(jnp.int32, (block, n), 1) - first
        inside = (across >= 0) & (across < block)
        given = jnp.where(inside, jnp.where(at == across, 1.0, 0.0), a[here, :])
        found = dot3(small, split(given), NN)
        high[here, :], low[here, :] = split(jnp.where(across < block, found, 0.0))
        finish(k)
        return found

    def step(k, carry):
        first = pl.multiple_of(k * block, block)
        after = pl.ds(pl.multiple_of(first + block, block), block)
        here = pl.ds(first, block)
        small = (high[here, here], low[here, here])
        left = split(dot3(split(a[after, here]), small, NT))
        corner = a[after, after] - dot3(left, left, NT)
        across = lax.broadcasted_iota(jnp.int32, (128, n), 1) - first
        inside = (across >= 0) & (across < block)
        turns = [2 * i for i in range(1, n // block)] + [n // block * 2 - 1]

        def beside(p):
            if p == 0:
                line[0], line[1] = split(make_line(k))
            if p == 1:
                columns[0], columns[1] = split(dot3(split(a[:, here]), small, NT))
            if p in turns:
                i0 = turns.index(p) * 128
                i1 = i0 + 128
                change = dot3((columns[0, i0:i1, :], columns[1, i0:i1, :]), (line[0], line[1]), NN)
                a[i0:i1, :] = jnp.where(inside, 0.0, a[i0:i1, :]) - change

        high[after, after], low[after, after] = factor_of(corner, beside)
        return carry

    high[0:block, 0:block], low[0:block, 0:block] = factor_of(corner, fill)
    lax.fori_loop(0, n // block - 1, step, 0)
    make_line(n // block - 1)


def panel_kernel(plan, samples_all, places, *refs):
    count = len(plan)
    pieces, (high_ref, low_ref, panel_ref, data, a, high, low, columns, line, in_sem, out_sem) = refs[:count], refs[count:]
    width, samples = data.shape
    copies = []
    for i, (piece, slots) in enumerate(zip(pieces, plan)):
        tall, depth = piece.shape[1:]
        place = pl.multiple_of(places[i], block)
        for t, slot in enumerate(slots):
            at = pl.multiple_of(places[count + slot] * depth, block)
            copies.append(
                pltpu.make_async_copy(piece.at[t], data.at[pl.ds(place, tall), pl.ds(at, depth)], in_sem)
            )
    for c in copies:
        c.start()
    for c in copies:
        c.wait()
    keep = pltpu.make_async_copy(data, panel_ref, out_sem)
    keep.start()
    step = 2 * block

    def linkage_rows(i0, tall, wide):
        part = dot1(data[i0 : i0 + tall, :], data[0:wide, :], NT) / samples_all
        at = lax.broadcasted_iota(jnp.int32, part.shape, 0) + i0
        across = lax.broadcasted_iota(jnp.int32, part.shape, 1)
        return part + jnp.where(at == across, ridge, 0.0)

    def fill(p):
        turns = block // sublanes * step // width
        if p % turns == 0:
            i0 = p // turns * step
            a[i0 : i0 + step, :] = linkage_rows(i0, step, width)

    def out_copies(k):
        here = pl.ds(pl.multiple_of(k * block, block), block)
        return [
            pltpu.make_async_copy(source.at[here, :], target.at[here, :], out_sem)
            for source, target in ((high, high_ref), (low, low_ref))
        ]

    def finish(k):
        for c in out_copies(k):
            c.start()

    invert_in_place(a, width, linkage_rows(0, block, block), fill, high, low, columns, line, finish)
    for k in range(width // block):
        for c in out_copies(k):
            c.wait()
    keep.wait()


def panel_step(pieces, plan, places, width, samples, samples_all):
    return pl.pallas_call(
        functools.partial(panel_kernel, plan, samples_all),
        out_shape=(
            jax.ShapeDtypeStruct((width, width), BF16),
            jax.ShapeDtypeStruct((width, width), BF16),
            jax.ShapeDtypeStruct((width, samples), BF16),
        ),
        in_specs=[pl.BlockSpec(memory_space=pltpu.SMEM)] + [pl.BlockSpec(memory_space=pl.ANY)] * len(pieces),
        out_specs=(pl.BlockSpec(memory_space=pl.ANY),) * 3,
        scratch_shapes=[
            pltpu.VMEM((width, samples), BF16),
            pltpu.VMEM((width, width), F32),
            pltpu.VMEM((width, width), BF16),
            pltpu.VMEM((width, width), BF16),
            pltpu.VMEM((2, width, block), BF16),
            pltpu.VMEM((2, block, width), BF16),
            pltpu.SemaphoreType.DMA,
            pltpu.SemaphoreType.DMA,
        ],
        compiler_params=pltpu.CompilerParams(vmem_limit_bytes=panel_vmem),
        cost_estimate=pl.CostEstimate(flops=40 * 10**9, bytes_accessed=20 * 2**20, transcendentals=0),
    )(places, *pieces)


def tile_kernel(samples_all, n_places, n_scores, col_plan, row_plan, facts, panel_ref, high_ref, low_ref, own_ref, *refs):
    score_refs, refs = refs[:n_scores], refs[n_scores:]
    pieces = refs[: len(col_plan)]
    cond_ref, whitened_ref, residual_ref, panel, cols, rows, high, low, change, sems = refs[-10:]
    extra = refs[len(col_plan) : -10]
    width, samples = panel.shape
    local_rows = rows.shape[0]
    row_place_panel = pl.multiple_of(facts[2], block)
    n_facts, slot_at = 5, 5 + n_places
    cols_own, rows_own = facts[0] == 1, facts[1] == 1
    load_panel = pltpu.make_async_copy(panel_ref, panel, sems.at[0])

    def copies(piece, target, first, plan, sem):
        tall, depth = piece.shape[1:]
        found = []
        for t, place, slot in plan:
            at = pl.multiple_of((facts[n_facts + place] if place >= 0 else 0) - first, block)
            across = pl.multiple_of(facts[slot_at + slot] * depth, block)
            found.append(
                pltpu.make_async_copy(piece.at[t], target.at[pl.ds(at, tall), pl.ds(across, depth)], sem)
            )
        return found

    def col_copies():
        return [c for p, plan in zip(pieces, col_plan) for c in copies(p, cols, 0, plan, sems.at[1])]

    def row_copies():
        if extra:
            return copies(extra[0], rows, 0, row_plan[0], sems.at[2])
        return [c for p, plan in zip(pieces, row_plan) for c in copies(p, rows, facts[2], plan, sems.at[2])]

    cols_from_panel = pltpu.make_async_copy(panel_ref, cols, sems.at[1])
    rows_from_panel = pltpu.make_async_copy(
        panel_ref.at[pl.ds(row_place_panel, local_rows), :], rows, sems.at[2]
    )

    @pl.when(rows_own)
    def _():
        rows_from_panel.start()

    @pl.when(jnp.logical_not(rows_own))
    def _():
        for c in row_copies():
            c.start()

    load_panel.start()
    loads = [
        pltpu.make_async_copy(source, target, sems.at[3]) for source, target in ((high_ref, high), (low_ref, low))
    ]
    for c in loads:
        c.start()
    @pl.when(cols_own)
    def _():
        cols_from_panel.start()

    @pl.when(jnp.logical_not(cols_own))
    def _():
        for c in col_copies():
            c.start()

    inverse = (high, low)
    step = 2 * block
    load_panel.wait()

    @pl.when(rows_own)
    def _():
        rows_from_panel.wait()

    @pl.when(jnp.logical_not(rows_own))
    def _():
        for c in row_copies():
            c.wait()

    tall = min(256, local_rows)
    chunks = [(r0, r0 + tall) for r0 in range(0, local_rows, tall)]
    tiles = [(j0, j0 + step) for j0 in range(0, width, step)]
    slabs = []
    for r0, r1 in chunks:
        slab = dot1(rows[r0:r1, :], panel[...], NT) / samples_all
        at = lax.broadcasted_iota(jnp.int32, slab.shape, 0) + (row_place_panel + r0)
        across = lax.broadcasted_iota(jnp.int32, slab.shape, 1)
        slabs.append(split(slab + jnp.where((at == across) & rows_own, ridge, 0.0)))
    for c in loads:
        c.wait()
    factors = []
    for slab in slabs:
        parts = [
            dot3(tuple(v[:, :j1] for v in slab), tuple(v[j0:j1, :j1] for v in inverse), NT) for j0, j1 in tiles
        ]
        factors.append(split(jnp.concatenate(parts, axis=1)))
    weights = []
    for (r0, r1), factor in zip(chunks, factors):
        parts = [
            dot3(tuple(v[:, j0:] for v in factor), tuple(v[j0:, j0:j1] for v in inverse), NN) for j0, j1 in tiles
        ]
        value = jnp.concatenate(parts, axis=1)
        cond_ref[r0:r1, :] = value
        weights.append(split(value))
    scores = score_refs[0][...]
    if n_scores == 2:
        beside = score_refs[1][...]
        first = row_place_panel == 0
        scores = jnp.concatenate([jnp.where(first, scores, beside), jnp.where(first, beside, scores)], axis=1)
    scores = split(scores)
    for j0, j1 in tiles:
        whitened_ref[:, j0:j1] = dot3(
            tuple(v[:, :j1] for v in scores), tuple(v[j0:j1, :j1] for v in inverse), NT
        )
    for (r0, r1), parts in zip(chunks, weights):
        both = jnp.concatenate([panel[...], panel[...]], axis=0)
        explained = dot1(jnp.concatenate(parts, axis=1), both, NN)
        change[r0:r1, :] = (rows[r0:r1, :].astype(F32) - explained).astype(BF16)
    whitened = split(whitened_ref[...])
    for (r0, r1), factor in zip(chunks, factors):
        residual_ref[:, r0:r1] = own_ref[:, r0:r1] - dot3(whitened, factor, NT)

    @pl.when(cols_own)
    def _():
        cols_from_panel.wait()

    @pl.when(jnp.logical_not(cols_own))
    def _():
        for c in col_copies():
            c.wait()

    row_first, col_first = facts[3], facts[4]
    for r0, r1 in chunks:
        part = dot1(change[r0:r1, :], cols[...], NT) / samples_all
        at = lax.broadcasted_iota(jnp.int32, part.shape, 0) + (row_first + r0)
        across = lax.broadcasted_iota(jnp.int32, part.shape, 1) + col_first
        unit = jnp.where(at == across, 1.0, 0.0)
        cond_ref[r0:r1, :] = part + ridge * (unit - jnp.where(cols_own, cond_ref[r0:r1, :], 0.0))


def tile_step(facts, panel, high, low, scores, own, pieces, n_places, col_plan, row_plan, extra, samples_all):
    width, samples = panel.shape
    traits, local_rows = own.shape
    smem = pl.BlockSpec(memory_space=pltpu.SMEM)
    vmem = pl.BlockSpec(memory_space=pltpu.VMEM)
    anywhere = pl.BlockSpec(memory_space=pl.ANY)
    return pl.pallas_call(
        functools.partial(tile_kernel, samples_all, n_places, len(scores), col_plan, row_plan),
        out_shape=(
            jax.ShapeDtypeStruct((local_rows, width), F32),
            jax.ShapeDtypeStruct((traits, width), F32),
            jax.ShapeDtypeStruct((traits, local_rows), F32),
        ),
        in_specs=[smem] + [anywhere] * 3 + [vmem] * (1 + len(scores)) + [anywhere] * (len(pieces) + len(extra)),
        out_specs=(vmem, vmem, vmem),
        scratch_shapes=[
            pltpu.VMEM((width, samples), BF16),
            pltpu.VMEM((width, samples), BF16),
            pltpu.VMEM((local_rows, samples), BF16),
            pltpu.VMEM((width, width), BF16),
            pltpu.VMEM((width, width), BF16),
            pltpu.VMEM((local_rows, samples), BF16),
            pltpu.SemaphoreType.DMA((4,)),
        ],
        compiler_params=pltpu.CompilerParams(vmem_limit_bytes=tile_vmem),
        cost_estimate=pl.CostEstimate(flops=20 * 10**9, bytes_accessed=20 * 2**20, transcendentals=0),
    )(facts, panel, high, low, own, *scores, *pieces, *extra)


swap = [(0, 1), (1, 0)]


def numbers(values):
    return jnp.stack([jnp.asarray(v).astype(jnp.int32) for v in values])


def standardized(genotypes, frequencies):
    spread = jnp.sqrt(2.0 * frequencies * (1.0 - frequencies))
    return ((genotypes.astype(F32) - 2.0 * frequencies) / spread).astype(BF16).T


def on_device(genotypes, frequencies, trait_scores, typed_mask, panel_index):
    n_samp, n_pan, n_mem, n_col = (lax.axis_size(a) for a in ("samp", "pan", "mem", "col"))
    samp, pan, mem, col = (lax.axis_index(a) for a in ("samp", "pan", "mem", "col"))
    depth, local_rows = genotypes.shape
    width = local_rows * n_mem
    samples_all = depth * n_samp
    q = panel_index[0] % n_col
    masked = trait_scores * typed_mask.astype(F32)
    own_panel = pan == q
    rest = []
    common = [col == q, own_panel, mem * local_rows, (pan * n_mem + mem) * local_rows, col * width]
    if n_pan == 2 and n_mem == 2 and n_col == 2 and n_samp == 4:
        quarter = local_rows // 4

        def part(i, j):
            at = (2 * i + j) * quarter
            return standardized(
                lax.dynamic_slice_in_dim(genotypes, at, quarter, 1), lax.dynamic_slice_in_dim(frequencies, at, quarter, 0)
            )

        mine, other = part(pan, col), lax.ppermute(part(1 - pan, col), "pan", swap)
        piece = jnp.where(own_panel, mine, other)
        rest_piece = jnp.where(own_panel, other, mine)

        def along_samp(v):
            steps = [[(s, (s + d) % n_samp) for s in range(n_samp)] for d in (1, 2, 3)]
            return [lax.ppermute(v, "samp", pairs) for pairs in steps]

        own = jnp.stack([piece] + along_samp(piece))
        panel_masked = jnp.where(own_panel, masked, lax.ppermute(masked, "pan", swap))
        corners = ((mem, pan), (1 - mem, pan), (mem, 1 - pan), (1 - mem, 1 - pan))
        slots = [(samp - d) % n_samp for d in range(n_samp)]

        def place(m, a, c):
            return (m * 4 + a * 2 + c) * quarter

        places = numbers([place(m, a, c) for c in (col, 1 - col) for m, a in corners] + slots)
        facts = numbers(common + [place(m, a, c) for c in (col, 1 - col) for m, a in corners] + slots)
        own, panel_masked, places, facts = lax.optimization_barrier((own, panel_masked, places, facts))
        beside = lax.ppermute(panel_masked, "mem", swap)
        by_mem, by_pan = lax.ppermute(own, "mem", swap), lax.ppermute(own, "pan", swap)
        cross = [(2 * i + j, 2 * (1 - i) + 1 - j) for i in range(2) for j in range(2)]
        far = lax.ppermute(own, ("pan", "mem"), cross)
        near = [own, by_mem, by_pan, far]
        twin = [lax.ppermute(v, "col", swap) for v in near]
        pieces = near + twin
        plan = [(0, 1, 2, 3)] * 8
        rest_piece, _ = lax.optimization_barrier((rest_piece, own))
        rest_own = jnp.stack([rest_piece] + along_samp(rest_piece))
        rest_own, _, _, beside = lax.optimization_barrier((rest_own, by_mem, by_pan, beside))
        rest = [
            rest_own,
            lax.ppermute(rest_own, "mem", swap),
            lax.ppermute(rest_own, "pan", swap),
            lax.ppermute(rest_own, ("pan", "mem"), cross),
        ]
        rest_twin = lax.ppermute(rest_own, "col", swap)
        col_plan = [[(d, t + 4 * c, d) for d in range(4)] for c in range(2) for t in range(4)]
        row_plan = [plan if i % 2 == 0 else [] for i, plan in enumerate(col_plan)]
        extra, n_places = [], 8
        panel_scores = [panel_masked, beside]
    else:
        standard = standardized(genotypes, frequencies)
        chosen = lax.psum(jnp.where(own_panel, standard, jnp.zeros_like(standard)), "pan")
        gathered = lax.all_gather(chosen, ("samp", "mem")).reshape(n_samp, width, depth)
        pieces, plan = [gathered], [tuple(range(n_samp))]
        places = [0, *range(n_samp)]
        cross = [(i * n_col + j, j * n_col + i) for i in range(n_pan) for j in range(n_col)]
        col_block = lax.ppermute(standard, ("pan", "col"), cross)
        col_pieces = [lax.all_gather(col_block, ("samp", "mem")).reshape(n_samp, width, depth)]
        extra, n_places = [lax.all_gather(standard, "samp")], 1
        col_plan = [[(s, 0, s) for s in range(n_samp)]]
        row_plan = [[(s, -1, s) for s in range(n_samp)]]
        facts = numbers(common + places)
        places = numbers(places)
        panel_masked = lax.psum(jnp.where(own_panel, masked, jnp.zeros_like(masked)), "pan")
        panel_scores = [lax.all_gather(panel_masked, "mem", axis=1, tiled=True)]
    high, low, panel_data = panel_step(pieces, plan, places, width, samples_all, samples_all)
    if rest:
        held = lax.optimization_barrier((high, *rest[1:]))
        high = held[0]
        rest = [rest[0], *held[1:]]
        col_pieces = rest + [rest_twin] + [lax.ppermute(v, "col", swap) for v in rest[1:]]
    return tile_step(
        facts, panel_data, high, low, panel_scores, masked, col_pieces, n_places, col_plan, row_plan, extra, samples_all
    )


def solution(mesh):
    n_samp, n_row, n_col = (mesh.shape[a] for a in ("samp", "row", "col"))
    inner = Mesh(mesh.devices.reshape(n_samp, n_col, n_row // n_col, n_col), ("samp", "pan", "mem", "col"))
    row = ("pan", "mem")
    return jax.shard_map(
        on_device,
        mesh=inner,
        in_specs=(P("samp", row), P(row), P(None, row), P(row), P()),
        out_specs=(P(row, "col"), P(), P(None, row)),
        check_vma=False,
    )
```
